32 devices in a mesh: lang: 16 (over z, y, x), rep: 2 (over core).
Axes of the slice: x: 2, y: 2, z: 4, core: 2. Of those that a mesh axis runs over, the one named last changes fastest.
Arguments:
- tokens: bfloat16 [4096, 1024], P(('lang', 'rep')), may hold values from -6 to 6
- grad_out: bfloat16 [4096, 1024], P(('lang', 'rep')), may hold values from -6 to 6
- lang_ids: int32 [4096], P(('lang', 'rep')), may hold values from 0 to 7, as said below
- slot_ids: int32 [4096], P(('lang', 'rep')), may hold values from 0 to 23, as said below
- w_up: bfloat16 [1024, 32768], P(None, 'lang'), may hold values from -0.1875 to 0.1875
- w_down_t: bfloat16 [1024, 32768], P(None, 'lang'), may hold values from -0.09375 to 0.09375
Outputs:
- ffn_out: bfloat16 [4096, 1024], P(('lang', 'rep'))
- grad_tokens: bfloat16 [4096, 1024], P(('lang', 'rep'))
- grad_up: float32 [1024, 32768], P('rep', 'lang')
- grad_down: float32 [1024, 32768], P('rep', 'lang')
The draws below stay inside these ranges and needn't reach their ends.
Inputs may be any that keep to these rules, and one draw needn't show every extreme that they name: `lang_ids`: each device holds 128 consecutive tokens. On every device one language, the same on all devices, has exactly 24 tokens; every other language has at most 18 tokens on a device, and on every device one of them has exactly 18. `slot_ids`: on each device the tokens of one language hold the distinct slots 0 to their count minus 1, in no particular order.
All inputs are finite; a program needn't handle non-finite values.
Results may differ from the reference program's by a relative error of at most 0.0058.
Values may be sent and summed in bfloat16 or wider, within the bound.
No kernel may reach another device: no remote copies, remote signals or barrier semaphores. Data moves between devices by JAX's collectives and lax.ppermute only.
A program may use at most 128 MiB of HBM per device.

```python
import jax
import jax.numpy as jnp
from jax import lax

D = 1024
HIDDEN_SIZE = 4096
MODULES = 8
TOK_DEV = 128
CAPACITY = 18
HOT = 24
TOKENS = 4096
N_LANG = 16


def routing(key):
    block_count = TOKENS // TOK_DEV
    hot_lang = jax.random.randint(jax.random.fold_in(key, 101), (), 0, MODULES).astype(jnp.int32)
    spread = TOK_DEV // 128
    remain = TOK_DEV - HOT - CAPACITY

    def one_block(block_key):
        key_jitter, key_langs, key_place, key_slots = jax.random.split(block_key, 4)
        jitter = jax.random.randint(key_jitter, (MODULES - 3,), -spread, spread + 1)
        cut_points = remain * jnp.arange(1, MODULES - 2) // (MODULES - 2) + jitter
        positions = jnp.arange(remain)
        ranked = 1 + jnp.sum(positions[:, None] >= cut_points[None, :], axis=1)
        ranked = jnp.concatenate([jnp.zeros((CAPACITY,), jnp.int32), ranked.astype(jnp.int32)])
        others = (hot_lang + 1 + jax.random.permutation(key_langs, MODULES - 1)) % MODULES
        rest_ids = jnp.take(others, ranked).astype(jnp.int32)
        ordered = jnp.concatenate([jnp.full((HOT,), hot_lang, jnp.int32), rest_ids])
        scores = jax.random.permutation(key_slots, TOK_DEV)
        same_lang = ordered[:, None] == ordered[None, :]
        slot_list = jnp.sum(same_lang & (scores[None, :] < scores[:, None]), axis=1).astype(jnp.int32)
        placing = jax.random.permutation(key_place, TOK_DEV)
        lang_row = jnp.zeros((TOK_DEV,), jnp.int32).at[placing].set(ordered)
        slot_row = jnp.zeros((TOK_DEV,), jnp.int32).at[placing].set(slot_list)
        return (lang_row, slot_row)

    def block_key_of(block_index):
        return jax.random.fold_in(key, block_index + 1000)
    block_keys = jax.vmap(block_key_of)(jnp.arange(block_count))
    lang_rows, slot_rows = jax.vmap(one_block)(block_keys)
    return (lang_rows.reshape(-1), slot_rows.reshape(-1))


def draw_lang_ids(key, part):
    return routing(key)[0]


def draw_slot_ids(key, part):
    return routing(key)[1]


def spiked(array, key, source, target, blocks, factor):
    def block_of(dim):
        return (jnp.arange(array.shape[dim]) // (array.shape[dim] // blocks)).reshape((-1,) + (1,) * (array.ndim - 1 - dim))

    near = jax.random.permutation(key, blocks)[block_of(target)]
    other_side = (block_of(target) + blocks // 2) % blocks
    return jnp.where((block_of(source) == near) | (block_of(source) == other_side), factor * array, array)


def steps_of(key, dims, pieces, least, largest):
    factor_of = 1.0
    for dim, blocks in pieces:
        draws = jax.random.uniform(jax.random.fold_in(jax.random.fold_in(key, 6), dim), (blocks,), jnp.float32, least / len(pieces), largest / len(pieces))
        factor_of = factor_of * jnp.repeat(jnp.exp(draws), dims[dim] // blocks).reshape((-1,) + (1,) * (len(dims) - 1 - dim))
    return factor_of


def noise(stream_key, dims, scale, most, cuts=(), kind=jnp.bfloat16):
    entries = scale * jax.random.normal(stream_key, dims, jnp.float32)
    if cuts:
        entries = entries * steps_of(stream_key, dims, cuts, -0.22, 0.18)
    return jnp.clip(entries, -most, most).astype(kind)


def heavy_noise(rng, dims, scale, most, pieces, heavy, kind=jnp.bfloat16):
    array = scale * jax.random.normal(rng, dims, jnp.float32)
    if pieces:
        array = array * steps_of(rng, dims, pieces, -0.22, 0.18)
    return jnp.clip(spiked(array, jax.random.fold_in(rng, 3), *heavy), -most, most).astype(kind)


def setup_inputs(seed: int = 0) -> dict:
    arg_keys = jax.random.split(jax.random.key(seed), 7)
    tokens = heavy_noise(arg_keys[0], (TOKENS, D), 1.0, 6.0, ((0, 32),), (0, 1, 32, 2.75))
    grad_out = heavy_noise(arg_keys[1], (TOKENS, D), 1.0, 6.0, ((0, 32),), (0, 1, 32, 2.75))
    lang_ids = draw_lang_ids(jax.random.fold_in(arg_keys[6], 71), 0)
    slot_ids = draw_slot_ids(jax.random.fold_in(arg_keys[6], 71), 0)
    w_up = noise(arg_keys[4], (D, MODULES * HIDDEN_SIZE), D ** -0.5, 0.1875, ((1, 16),))
    w_down_t = noise(arg_keys[5], (D, MODULES * HIDDEN_SIZE), HIDDEN_SIZE ** -0.5, 0.09375, ((1, 16),))
    return dict(tokens=tokens, grad_out=grad_out, lang_ids=lang_ids, slot_ids=slot_ids, w_up=w_up, w_down_t=w_down_t)


INV_ROOT_TWO = 0.7071067811865476
INV_ROOT_TAU = 0.3989422804014327


def gelu_value(values):
    return 0.5 * values * (1.0 + lax.erf(values * INV_ROOT_TWO))


def gelu_slope(values):
    return 0.5 * (1.0 + lax.erf(values * INV_ROOT_TWO)) + values * jnp.exp(-0.5 * values * values) * INV_ROOT_TAU


def reference(tokens, grad_out, lang_ids, slot_ids, w_up, w_down_t):
    groups = N_LANG // MODULES
    block_units = HIDDEN_SIZE // groups
    block_count = TOKENS // TOK_DEV
    keep_mask = slot_ids < CAPACITY
    target = jnp.where(keep_mask, lang_ids * CAPACITY + slot_ids, MODULES * CAPACITY).astype(jnp.int32)
    places = target.reshape(block_count, TOK_DEV)

    def place_one(block_vals, block_index):
        return jnp.zeros((MODULES * CAPACITY, D), block_vals.dtype).at[block_index].set(block_vals, mode="drop")

    def dispatch(values):
        filled = jax.vmap(place_one)(values.reshape(block_count, TOK_DEV, D), places)
        filled = filled.reshape(block_count, MODULES, CAPACITY, D).transpose(1, 0, 2, 3)
        return filled.reshape(MODULES, block_count * CAPACITY, D)

    up_stack = w_up.reshape(D, MODULES, HIDDEN_SIZE).transpose(1, 0, 2)
    down_stack = w_down_t.reshape(D, MODULES, HIDDEN_SIZE).transpose(1, 0, 2)

    def module_step(operands):
        module_x, module_dy, weight_up, weight_down = operands
        pre_act = jnp.dot(module_x, weight_up, preferred_element_type=jnp.float32)
        hidden = gelu_value(pre_act).astype(jnp.bfloat16)
        d_hidden = jnp.dot(module_dy, weight_down, preferred_element_type=jnp.float32)
        d_pre = (d_hidden * gelu_slope(pre_act)).astype(jnp.bfloat16)
        out_sum = jnp.zeros((module_x.shape[0], D), jnp.float32)
        dx_sum = jnp.zeros((module_x.shape[0], D), jnp.float32)
        for block_index in range(groups):
            low_unit = block_index * block_units
            high_unit = low_unit + block_units
            part_out = jnp.dot(hidden[:, low_unit:high_unit], weight_down[:, low_unit:high_unit].T, preferred_element_type=jnp.float32).astype(jnp.bfloat16)
            part_dx = jnp.dot(d_pre[:, low_unit:high_unit], weight_up[:, low_unit:high_unit].T, preferred_element_type=jnp.float32).astype(jnp.bfloat16)
            part_out = lax.optimization_barrier(part_out)
            part_dx = lax.optimization_barrier(part_dx)
            out_sum = out_sum + part_out.astype(jnp.float32)
            dx_sum = dx_sum + part_dx.astype(jnp.float32)
        grad_down = jnp.dot(module_dy.T, hidden, preferred_element_type=jnp.float32) * (1.0 / TOK_DEV)
        grad_up = jnp.dot(module_x.T, d_pre, preferred_element_type=jnp.float32) * (1.0 / TOK_DEV)
        return out_sum.astype(jnp.bfloat16), dx_sum.astype(jnp.bfloat16), grad_up, grad_down

    results = lax.map(module_step, (dispatch(tokens), dispatch(grad_out), up_stack, down_stack))
    safe_index = jnp.minimum(target, MODULES * CAPACITY - 1).astype(jnp.int32).reshape(block_count, TOK_DEV)

    def take_rows(all_rows, row_index):
        return jnp.take(all_rows, row_index, axis=0)

    def undispatch(per_module):
        filled = per_module.reshape(MODULES, block_count, CAPACITY, D).transpose(1, 0, 2, 3)
        filled = filled.reshape(block_count, MODULES * CAPACITY, D)
        picked = jax.vmap(take_rows)(filled, safe_index).reshape(TOKENS, D)
        return jnp.where(keep_mask[:, None], picked, jnp.zeros_like(picked))

    ffn_out = undispatch(results[0])
    grad_tokens = undispatch(results[1])
    grad_up = results[2].transpose(1, 0, 2).reshape(D, MODULES * HIDDEN_SIZE)
    grad_down = results[3].transpose(1, 0, 2).reshape(D, MODULES * HIDDEN_SIZE)
    return ffn_out, grad_tokens, grad_up, grad_down
```

```python
import jax
import jax.numpy as jnp
from jax import lax
from jax.sharding import PartitionSpec as P

MODULES = 8
TOK_DEV = 128
CAPACITY = 18
MAIN = 16
LANES = 128

INV_ROOT_TWO = 0.7071067811865476
INV_ROOT_TAU = 0.3989422804014327


def gelu_value(values):
    return 0.5 * values * (1.0 + lax.erf(values * INV_ROOT_TWO))


def gelu_slope(values):
    return (
        0.5 * (1.0 + lax.erf(values * INV_ROOT_TWO))
        + values * jnp.exp(-0.5 * values * values) * INV_ROOT_TAU
    )


def dot(a, b, contract):
    return lax.dot_general(a, b, (contract, ((), ())), preferred_element_type=jnp.float32)


def per_device(tokens, grad_out, lang_ids, slot_ids, w_up, w_down_t):
    n_lang = lax.axis_size("lang")
    n_rep = lax.axis_size("rep")
    groups = n_lang // MODULES
    count, width = tokens.shape
    pieces = width // LANES
    spare = CAPACITY - MAIN
    rows = MODULES * MAIN
    scale = 1.0 / TOK_DEV

    row = lax.broadcasted_iota(jnp.int32, (rows, count), 0)
    lang, place = row // MAIN, row % MAIN
    here = lang == lang_ids[None, :]
    slots = slot_ids[None, :]
    pick_main = (here & (slots == place)).astype(jnp.bfloat16)
    in_spare = here & (slots == MAIN + place // pieces)
    pick_spare = [(in_spare & (place % pieces == p)).astype(jnp.bfloat16) for p in range(pieces)]

    def pack(values):
        main = dot(pick_main, values, ((1,), (0,)))
        extra = sum(
            dot(pick_spare[p], values[:, p * LANES : (p + 1) * LANES], ((1,), (0,)))
            for p in range(pieces)
        )
        return jnp.concatenate([main, extra], axis=1).astype(jnp.bfloat16)

    def collect(packed):
        main = dot(pick_main, packed[:, :width], ((0,), (0,)))
        extra = jnp.concatenate(
            [dot(pick_spare[p], packed[:, width:], ((0,), (0,))) for p in range(pieces)], axis=1
        )
        return (main + extra).astype(jnp.bfloat16)

    def unpack(packed):
        extra = packed[:, width:].reshape(MODULES * spare, width)
        return jnp.concatenate([packed[:, :width], extra], axis=0)

    def repack(full):
        extra = full[rows:].reshape(rows, LANES)
        return jnp.concatenate([full[:rows], extra], axis=1)

    planes = [[g + groups * m for m in range(MODULES)] for g in range(groups)]

    def exchange(packed):
        cut = packed.reshape(MODULES, MAIN, packed.shape[1])
        got = lax.all_to_all(
            cut, "lang", split_axis=0, concat_axis=0, axis_index_groups=planes, tiled=True
        )
        return got.reshape(packed.shape)

    def shift_group(value, step):
        pairs = [
            (m * groups + g, m * groups + (g + step) % groups)
            for m in range(MODULES)
            for g in range(groups)
        ]
        return lax.ppermute(value, "lang", pairs)

    def shift_rep(value, step):
        return lax.ppermute(value, "rep", [(r, (r + step) % n_rep) for r in range(n_rep)])

    def spread(packed):
        return [packed] + [shift_group(packed, s) for s in range(1, groups)]

    def gather_rows(parts):
        return jnp.concatenate([unpack(p) for p in parts], axis=0)

    def reduce_group(partial):
        part_rows = rows + MODULES * spare
        parts = [partial[s * part_rows : (s + 1) * part_rows] for s in range(groups)]
        total = repack(parts[0]).astype(jnp.float32)
        for s in range(1, groups):
            total = total + shift_group(repack(parts[s]), -s).astype(jnp.float32)
        return total.astype(jnp.bfloat16)

    x_rows = gather_rows(spread(exchange(pack(tokens))))
    y_rows = gather_rows(spread(exchange(pack(grad_out))))

    pre = dot(x_rows, w_up, ((1,), (0,)))
    hidden = gelu_value(pre).astype(jnp.bfloat16)
    out_part = dot(hidden, w_down_t, ((1,), (1,))).astype(jnp.bfloat16)
    out_back = exchange(reduce_group(out_part))

    d_hidden = dot(y_rows, w_down_t, ((1,), (0,)))
    d_pre = (d_hidden * gelu_slope(pre)).astype(jnp.bfloat16)
    dx_part = dot(d_pre, w_up, ((1,), (1,))).astype(jnp.bfloat16)
    dx_back = exchange(reduce_group(dx_part))

    own = width // n_rep
    start = lax.axis_index("rep") * own

    def over_reps(value):
        return [value] + [shift_rep(value, s) for s in range(1, n_rep)]

    def weight_grad(left, right):
        lefts = jnp.concatenate(over_reps(left), axis=0)
        lefts = lax.dynamic_slice_in_dim(lefts, start, own, axis=1)
        rights = jnp.concatenate(over_reps(right), axis=0)
        return dot(lefts, rights, ((0,), (0,))) * scale

    grad_down = weight_grad(y_rows, hidden)
    grad_up = weight_grad(x_rows, d_pre)
    return collect(out_back), collect(dx_back), grad_up, grad_down


def solution(mesh):
    placed = (
        P(("lang", "rep"), None),
        P(("lang", "rep"), None),
        P(("lang", "rep")),
        P(("lang", "rep")),
        P(None, "lang"),
        P(None, "lang"),
    )
    return jax.shard_map(
        per_device,
        mesh=mesh,
        in_specs=placed,
        out_specs=(
            P(("lang", "rep"), None),
            P(("lang", "rep"), None),
            P("rep", "lang"),
            P("rep", "lang"),
        ),
        check_vma=False,
    )
```

```python
import functools

import jax
import jax.numpy as jnp
from jax import lax
from jax.experimental import pallas as pl
from jax.experimental.pallas import tpu as pltpu
from jax.sharding import PartitionSpec as P

MODULES = 8
TOK_DEV = 128
CAPACITY = 18
MAIN = 16
LANES = 128
SPARE = CAPACITY - MAIN
ROWS = MODULES * MAIN
PART = MODULES * CAPACITY

INV_ROOT_TWO = 0.7071067811865476
INV_ROOT_TAU = 0.3989422804014327


def gelu_value(values):
    return 0.5 * values * (1.0 + lax.erf(values * INV_ROOT_TWO))


def gelu_slope(values):
    return (
        0.5 * (1.0 + lax.erf(values * INV_ROOT_TWO))
        + values * jnp.exp(-0.5 * values * values) * INV_ROOT_TAU
    )


def dot(a, b, contract):
    return lax.dot_general(a, b, (contract, ((), ())), preferred_element_type=jnp.float32)


def piece_order():
    place = lax.broadcasted_iota(jnp.int32, (LANES, LANES), 0)
    column = lax.broadcasted_iota(jnp.int32, (LANES, LANES), 1)
    return ((place & 15) * 8 + (place >> 4) == column).astype(jnp.bfloat16)


def spare_rows(cut):
    ordered = dot(piece_order(), cut, ((1,), (0,))).astype(jnp.bfloat16)
    return jnp.concatenate([ordered[16 * p : 16 * (p + 1)] for p in range(8)], axis=1)


def spare_cut(rows):
    ordered = jnp.concatenate([rows[:, LANES * p : LANES * (p + 1)] for p in range(8)], axis=0)
    return dot(piece_order(), ordered, ((0,), (0,))).astype(jnp.bfloat16)


def slot_picks(lang_ref, slot_ref):
    count = lang_ref.shape[1]
    row = lax.broadcasted_iota(jnp.int32, (PART, count), 0)
    is_main = row < ROWS
    lang = jnp.where(is_main, row >> 4, (row - ROWS) >> 1)
    slot = jnp.where(is_main, row & 15, MAIN + (row & 1))
    hit = (lang == lang_ref[...]) & (slot == slot_ref[...])
    return hit.astype(jnp.bfloat16)


def pack_kernel(lang_ref, slot_ref, values_ref, packed_ref):
    width = values_ref.shape[1]
    rows = dot(slot_picks(lang_ref, slot_ref), values_ref[...], ((1,), (0,))).astype(jnp.bfloat16)
    packed_ref[:, :width] = rows[:ROWS]
    packed_ref[:, width:] = spare_cut(rows[ROWS:])


def unpack_kernel(packed_ref, rows_ref):
    width = rows_ref.shape[1]
    rows_ref[:ROWS] = packed_ref[:, :width]
    rows_ref[ROWS:] = spare_rows(packed_ref[:, width:])


def sum_pack_kernel(*refs):
    packed_ref = refs[-1]
    total = refs[0][...].astype(jnp.float32)
    for ref in refs[1:-1]:
        total = total + ref[...].astype(jnp.float32)
    total = total.astype(jnp.bfloat16)
    width = total.shape[1]
    packed_ref[:, :width] = total[:ROWS]
    packed_ref[:, width:] = spare_cut(total[ROWS:])


def collect_kernel(lang_ref, slot_ref, packed_ref, values_ref):
    width = values_ref.shape[1]
    rows = jnp.concatenate([packed_ref[:, :width], spare_rows(packed_ref[:, width:])], axis=0)
    picked = dot(slot_picks(lang_ref, slot_ref), rows, ((0,), (0,)))
    values_ref[...] = picked.astype(jnp.bfloat16)


def weight_grad_kernel(n_parts, start_ref, *refs):
    lefts, rights = refs[:n_parts], refs[n_parts : 2 * n_parts]
    out_ref, turned = refs[2 * n_parts :]
    own = out_ref.shape[0]

    @pl.when(pl.program_id(0) == 0)
    def _():
        columns = pl.ds(pl.multiple_of(start_ref[0], LANES), own)
        left = jnp.concatenate([ref[:, columns] for ref in lefts], axis=0)
        turned[...] = left.T

    right = jnp.concatenate([ref[...] for ref in rights], axis=0)
    out_ref[...] = dot(turned[...], right, ((1,), (0,))) * (1.0 / TOK_DEV)


def in_vmem(kernel, out_shape, cost=0):
    return pl.pallas_call(
        kernel,
        out_shape=out_shape,
        cost_estimate=pl.CostEstimate(flops=cost, bytes_accessed=1 << 20, transcendentals=0),
    )


def weight_grad(start, lefts, rights, own):
    n_parts = len(lefts)
    units = rights[0].shape[1]
    depth = sum(left.shape[0] for left in lefts)
    tile = min(512, units)
    if n_parts > 4:
        left = lax.dynamic_slice_in_dim(jnp.concatenate(lefts, axis=0), start, own, axis=1)
        return dot(left, jnp.concatenate(rights, axis=0), ((0,), (0,))) * (1.0 / TOK_DEV)
    return pl.pallas_call(
        functools.partial(weight_grad_kernel, n_parts),
        out_shape=jax.ShapeDtypeStruct((own, units), jnp.float32),
        grid=(units // tile,),
        in_specs=[pl.BlockSpec(memory_space=pltpu.SMEM)]
        + [pl.BlockSpec(left.shape, lambda i: (0, 0)) for left in lefts]
        + [pl.BlockSpec((right.shape[0], tile), lambda i: (0, i)) for right in rights],
        out_specs=pl.BlockSpec((own, tile), lambda i: (0, i)),
        scratch_shapes=[pltpu.VMEM((own, depth), jnp.bfloat16)],
        cost_estimate=pl.CostEstimate(
            flops=2 * own * depth * units, bytes_accessed=4 * own * units, transcendentals=0
        ),
        compiler_params=pltpu.CompilerParams(vmem_limit_bytes=24 << 20),
    )(start.reshape(1), *lefts, *rights)


def per_device(tokens, grad_out, lang_ids, slot_ids, w_up, w_down_t):
    n_lang = lax.axis_size("lang")
    n_rep = lax.axis_size("rep")
    groups = n_lang // MODULES
    count, width = tokens.shape
    lang_row, slot_row = lang_ids.reshape(1, count), slot_ids.reshape(1, count)
    packed_shape = jax.ShapeDtypeStruct((ROWS, width + LANES), jnp.bfloat16)
    rows_shape = jax.ShapeDtypeStruct((PART, width), jnp.bfloat16)
    values_shape = jax.ShapeDtypeStruct((count, width), jnp.bfloat16)
    planes = [[g + groups * m for m in range(MODULES)] for g in range(groups)]

    def pack(values):
        return in_vmem(pack_kernel, packed_shape)(lang_row, slot_row, values)

    def exchange(packed):
        cut = packed.reshape(MODULES, MAIN, packed.shape[1])
        got = lax.all_to_all(
            cut, "lang", split_axis=0, concat_axis=0, axis_index_groups=planes, tiled=True
        )
        return got.reshape(packed.shape)

    def shift_group(value, step):
        pairs = [
            (m * groups + g, m * groups + (g + step) % groups)
            for m in range(MODULES)
            for g in range(groups)
        ]
        return lax.ppermute(value, "lang", pairs)

    def shift_rep(value, step):
        return lax.ppermute(value, "rep", [(r, (r + step) % n_rep) for r in range(n_rep)])

    def spread(packed):
        rows = in_vmem(unpack_kernel, rows_shape)(packed)
        return [rows] + [shift_group(rows, s) for s in range(1, groups)]

    def send_back(parts):
        sums = [parts[0]] + [shift_group(parts[s], -s) for s in range(1, groups)]
        return exchange(in_vmem(sum_pack_kernel, packed_shape)(*sums))

    def collect(packed):
        return in_vmem(collect_kernel, values_shape)(lang_row, slot_row, packed)

    x_parts = spread(exchange(pack(tokens)))
    y_parts = spread(exchange(pack(grad_out)))

    pre = [dot(x, w_up, ((1,), (0,))) for x in x_parts]
    hidden = [gelu_value(v).astype(jnp.bfloat16) for v in pre]
    out_parts = [dot(h, w_down_t, ((1,), (1,))).astype(jnp.bfloat16) for h in hidden]
    out_back = send_back(out_parts)

    d_hidden = [dot(y, w_down_t, ((1,), (0,))) for y in y_parts]
    d_pre = [(d * gelu_slope(v)).astype(jnp.bfloat16) for d, v in zip(d_hidden, pre)]
    dx_parts = [dot(d, w_up, ((1,), (1,))).astype(jnp.bfloat16) for d in d_pre]
    dx_back = send_back(dx_parts)

    own = width // n_rep
    start = lax.axis_index("rep") * own

    def over_reps(parts):
        return [shift_rep(v, s) if s else v for s in range(n_rep) for v in parts]

    grad_down = weight_grad(start, over_reps(y_parts), over_reps(hidden), own)
    grad_up = weight_grad(start, over_reps(x_parts), over_reps(d_pre), own)
    return collect(out_back), collect(dx_back), grad_up, grad_down


def solution(mesh):
    placed = (
        P(("lang", "rep"), None),
        P(("lang", "rep"), None),
        P(("lang", "rep")),
        P(("lang", "rep")),
        P(None, "lang"),
        P(None, "lang"),
    )
    return jax.shard_map(
        per_device,
        mesh=mesh,
        in_specs=placed,
        out_specs=(
            P(("lang", "rep"), None),
            P(("lang", "rep"), None),
            P("rep", "lang"),
            P("rep", "lang"),
        ),
        check_vma=False,
    )
```

```python
import functools

import jax
import jax.numpy as jnp
from jax import lax
from jax.experimental import pallas as pl
from jax.experimental.pallas import tpu as pltpu
from jax.sharding import PartitionSpec as P

MODULES = 8
TOK_DEV = 128
CAPACITY = 18
MAIN = 16
PACK_LIMIT = 60
LANES = 128
SPARE = CAPACITY - MAIN
ROWS = MODULES * MAIN
PART = MODULES * CAPACITY

INV_ROOT_TWO = 0.7071067811865476
INV_ROOT_TAU = 0.3989422804014327


def gelu_share(values):
    return 0.5 * (1.0 + lax.erf(values * INV_ROOT_TWO))


def dot(a, b, contract):
    return lax.dot_general(a, b, (contract, ((), ())), preferred_element_type=jnp.float32)


def piece_order():
    place = lax.broadcasted_iota(jnp.int32, (LANES, LANES), 0)
    column = lax.broadcasted_iota(jnp.int32, (LANES, LANES), 1)
    return ((place & 15) * 8 + (place >> 4) == column).astype(jnp.bfloat16)


def spare_rows(cut):
    ordered = dot(piece_order(), cut, ((1,), (0,))).astype(jnp.bfloat16)
    return jnp.concatenate([ordered[16 * p : 16 * (p + 1)] for p in range(8)], axis=1)


def spare_cut(rows):
    ordered = jnp.concatenate([rows[:, LANES * p : LANES * (p + 1)] for p in range(8)], axis=0)
    return dot(piece_order(), ordered, ((0,), (0,))).astype(jnp.bfloat16)


def slot_picks(lang, slot):
    row = lax.broadcasted_iota(jnp.int32, (PART, lang.shape[1]), 0)
    is_main = row < ROWS
    block = jnp.where(is_main, row >> 4, (row - ROWS) >> 1)
    place = jnp.where(is_main, row & 15, MAIN + (row & 1))
    return ((block == lang) & (place == slot)).astype(jnp.bfloat16)


def pack_kernel(me_ref, *refs):
    sources, outs, staged, arrived = refs[:4], refs[4:9], refs[9:13], refs[13]
    copies = [
        pltpu.make_async_copy(source, stage, arrived.at[i])
        for i, (source, stage) in enumerate(zip(sources, staged))
    ]
    for copy in copies:
        copy.start()
    for copy in copies[:3]:
        copy.wait()
    lang, slot = staged[0][...], staged[1][...]
    width = staged[2].shape[1]
    rows, cut = packed_rows(slot_picks(lang ^ me_ref[0], slot), staged[2][...])
    for z, out_ref in enumerate(outs[:4]):
        out_ref[:, :width] = rows[32 * z : 32 * (z + 1)]
        out_ref[:, width:] = cut[32 * z : 32 * (z + 1)]
    copies[3].wait()
    outs[4][:, :width], outs[4][:, width:] = packed_rows(slot_picks(lang, slot), staged[3][...])


def packed_rows(picks, values):
    rows = dot(picks, values, ((1,), (0,))).astype(jnp.bfloat16)
    return rows[:ROWS], spare_cut(rows[ROWS:])


def split_kernel(*refs):
    low_ref, high_ref = refs[-2:]
    for z, message_ref in enumerate(refs[:-2]):
        low_ref[16 * z : 16 * (z + 1)] = message_ref[:16]
        high_ref[16 * z : 16 * (z + 1)] = message_ref[16:]


def split_kernel(*refs):
    messages, outs = refs[:4], refs[4:]
    for z, message_ref in enumerate(messages):
        for place, out_ref in enumerate(outs):
            out_ref[16 * z : 16 * (z + 1)] = message_ref[16 * place : 16 * (place + 1)]


NEAR = (0, 2, 4, 6, 1, 3, 5, 7)


def put_rows(packed, rows_ref, first):
    width = rows_ref.shape[1]
    rows_ref[first : first + ROWS] = packed[:, :width]
    rows_ref[first + ROWS : first + PART] = spare_rows(packed[:, width:])


def unpack_near_kernel(groups, *refs):
    for g in range(groups):
        packed = jnp.concatenate([refs[g][...], refs[groups + g][...]], axis=0)
        put_rows(packed, refs[-1], PART * g)


def unpack_kernel(me_ref, *refs):
    for g, packed_ref in enumerate(refs[:-1]):
        blocks = [
            packed_ref[pl.ds(pl.multiple_of((me_ref[0] ^ near) * MAIN, MAIN), MAIN)] for near in NEAR
        ]
        put_rows(jnp.concatenate(blocks, axis=0), refs[-1], PART * g)


def put_packed(rows, packed_ref, place_of):
    width = rows.shape[1]
    cut = spare_cut(rows[ROWS:])
    for j, near in enumerate(NEAR):
        at = pl.ds(pl.multiple_of(place_of(near) * MAIN, MAIN), MAIN)
        packed_ref[at, :width] = rows[MAIN * j : MAIN * (j + 1)]
        packed_ref[at, width:] = cut[MAIN * j : MAIN * (j + 1)]


def sum_pack_kernel(me_ref, *refs):
    total = refs[0][...].astype(jnp.float32)
    for ref in refs[1:-1]:
        total = total + ref[...].astype(jnp.float32)
    put_packed(total.astype(jnp.bfloat16), refs[-1], lambda near: me_ref[0] ^ near)


def pack_all_kernel(groups, me_ref, member_ref, rows_ref, packed_ref):
    for s in range(groups):
        member = lax.rem(member_ref[0] + groups - s, groups)
        put_packed(
            rows_ref[PART * s : PART * (s + 1)],
            packed_ref,
            lambda near, member=member: (me_ref[0] ^ near) * groups + member,
        )


def collect_kernel(terms, lang_ref, slot_ref, packed_ref, values_ref):
    width = values_ref.shape[1]
    picks = slot_picks(lang_ref[...], slot_ref[...])
    packed = packed_ref[...]
    if terms > 1:
        total = packed.astype(jnp.float32).reshape(MODULES, terms, MAIN, width + LANES)
        packed = sum(total[:, g] for g in range(terms)).reshape(ROWS, width + LANES)
        packed = packed.astype(jnp.bfloat16)
    rows = jnp.concatenate([packed[:, :width], spare_rows(packed[:, width:])], axis=0)
    values_ref[...] = dot(picks, rows, ((0,), (0,))).astype(jnp.bfloat16)


def weight_grad_kernel(n_parts, start_ref, *refs):
    lefts, rights = refs[:n_parts], refs[n_parts : 2 * n_parts]
    out_ref, turned = refs[2 * n_parts :]
    own, tile = out_ref.shape
    step = pl.program_id(0)

    @pl.when(step == 0)
    def _():
        columns = pl.ds(pl.multiple_of(start_ref[0], LANES), own)
        turned[...] = jnp.concatenate([ref[:, columns] for ref in lefts], axis=0).T

    units = pl.ds(pl.multiple_of(step * tile, LANES), tile)
    right = jnp.concatenate([ref[:, units] for ref in rights], axis=0)
    out_ref[...] = dot(turned[...], right, ((1,), (0,))) * (1.0 / TOK_DEV)


VMEM_SPEC = pl.BlockSpec(memory_space=pltpu.VMEM)
SMEM_SPEC = pl.BlockSpec(memory_space=pltpu.SMEM)
FREE = pl.CostEstimate(flops=0, bytes_accessed=0, transcendentals=0)


def shapes_of(shapes):
    return [jax.ShapeDtypeStruct(shape, jnp.bfloat16) for shape in shapes]


def local(kernel, shapes, *operands, scalars=0):
    return pl.pallas_call(
        kernel,
        out_shape=shapes_of(shapes),
        in_specs=[SMEM_SPEC] * scalars + [VMEM_SPEC] * (len(operands) - scalars),
        out_specs=[VMEM_SPEC] * len(shapes),
        cost_estimate=FREE,
        compiler_params=pltpu.CompilerParams(vmem_limit_bytes=4 << 20),
    )(*operands)


def pack(me, lang_row, slot_row, tokens, grad_out):
    sources = (lang_row, slot_row, tokens, grad_out)
    packed_width = tokens.shape[1] + LANES
    return pl.pallas_call(
        pack_kernel,
        out_shape=shapes_of([(32, packed_width)] * 4 + [(ROWS, packed_width)]),
        in_specs=[SMEM_SPEC] + [pl.BlockSpec(memory_space=pltpu.HBM)] * 4,
        out_specs=[VMEM_SPEC] * 5,
        scratch_shapes=[pltpu.VMEM(v.shape, v.dtype) for v in sources]
        + [pltpu.SemaphoreType.DMA((4,))],
        cost_estimate=FREE,
        compiler_params=pltpu.CompilerParams(vmem_limit_bytes=PACK_LIMIT << 20),
    )(me, *sources)


def after(values, *earlier):
    return lax.optimization_barrier((*values, *earlier))[: len(values)]


def weight_grad(start, lefts, rights, own):
    n_parts = len(lefts)
    units = rights[0].shape[1]
    depth = sum(left.shape[0] for left in lefts)
    tile = min(512, units)
    if n_parts > 4:
        left = lax.dynamic_slice_in_dim(jnp.concatenate(lefts, axis=0), start, own, axis=1)
        return dot(left, jnp.concatenate(rights, axis=0), ((0,), (0,))) * (1.0 / TOK_DEV)
    return pl.pallas_call(
        functools.partial(weight_grad_kernel, n_parts),
        out_shape=jax.ShapeDtypeStruct((own, units), jnp.float32),
        grid=(units // tile,),
        in_specs=[SMEM_SPEC] + [VMEM_SPEC] * (2 * n_parts),
        out_specs=pl.BlockSpec((own, tile), lambda i: (0, i)),
        scratch_shapes=[pltpu.VMEM((own, depth), jnp.bfloat16)],
        cost_estimate=pl.CostEstimate(
            flops=2 * own * depth * units, bytes_accessed=4 * own * units, transcendentals=0
        ),
        compiler_params=pltpu.CompilerParams(vmem_limit_bytes=12 << 20),
    )(start.reshape(1), *lefts, *rights)


def per_device(tokens, grad_out, lang_ids, slot_ids, w_up, w_down_t):
    n_lang = lax.axis_size("lang")
    n_rep = lax.axis_size("rep")
    groups = n_lang // MODULES
    count, width = tokens.shape
    lang_index = lax.axis_index("lang")
    me = (lang_index // groups).astype(jnp.int32).reshape(1)
    member = lax.rem(lang_index, groups).astype(jnp.int32).reshape(1)
    lang_row, slot_row = lang_ids.reshape(1, count), slot_ids.reshape(1, count)
    packed_width = width + LANES

    def shift_near(value, bits):
        pairs = [
            (m * groups + g, (m ^ bits) * groups + g) for m in range(MODULES) for g in range(groups)
        ]
        return lax.ppermute(value, "lang", pairs)

    def shift_group(value, step):
        pairs = [
            (m * groups + g, m * groups + (g + step) % groups)
            for m in range(MODULES)
            for g in range(groups)
        ]
        return lax.ppermute(value, "lang", pairs)

    def shift_rep(value, step):
        return lax.ppermute(value, "rep", [(r, (r + step) % n_rep) for r in range(n_rep)])

    def over_groups(value):
        return [value] + [shift_group(value, s) for s in range(1, groups)]

    def exchange(packed):
        planes = [[g + groups * m for m in range(MODULES)] for g in range(groups)]
        cut = packed.reshape(MODULES, MAIN, packed_width)
        got = lax.all_to_all(
            cut, "lang", split_axis=0, concat_axis=0, axis_index_groups=planes, tiled=True
        )
        return got.reshape(ROWS, packed_width)

    def exchange_all(packed):
        cut = packed.reshape(n_lang, MAIN, packed_width)
        got = lax.all_to_all(cut, "lang", split_axis=0, concat_axis=0, tiled=True)
        return got.reshape(packed.shape)

    def collect(packed, terms):
        kernel = functools.partial(collect_kernel, terms)
        return local(kernel, [(count, width)], lang_row, slot_row, packed)[0]

    *x_messages, y_packed = pack(me, lang_row, slot_row, tokens, grad_out)

    got = [x_messages[0]] + [shift_near(x_messages[z], 2 * z) for z in (1, 2, 3)]
    x_low, x_send = local(split_kernel, [(64, packed_width)] * 2, *got)
    x_high = shift_near(x_send, 1)
    x_rows = local(
        functools.partial(unpack_near_kernel, groups),
        [(groups * PART, width)],
        *over_groups(x_low),
        *over_groups(x_high),
    )[0]
    y_rows = local(
        unpack_kernel, [(groups * PART, width)], me, *over_groups(exchange(y_packed)), scalars=1
    )[0]

    pre = dot(x_rows, w_up, ((1,), (0,)))
    share = gelu_share(pre)
    hidden = (pre * share).astype(jnp.bfloat16)
    slope = share + pre * jnp.exp(-0.5 * pre * pre) * INV_ROOT_TAU
    hidden, slope = lax.optimization_barrier((hidden, slope))
    out = dot(hidden, w_down_t, ((1,), (1,))).astype(jnp.bfloat16)
    out_packed = local(
        functools.partial(pack_all_kernel, groups),
        [(groups * ROWS, packed_width)],
        me,
        member,
        out,
        scalars=2,
    )[0]
    out_back = exchange_all(out_packed)
    ffn_out = collect(out_back, groups)

    (y_rows,) = after((y_rows,), out_packed)
    d_pre = (dot(y_rows, w_down_t, ((1,), (0,))) * slope).astype(jnp.bfloat16)
    dx = dot(d_pre, w_up, ((1,), (1,))).astype(jnp.bfloat16)
    dx_parts = [dx[PART * g : PART * (g + 1)] for g in range(groups)]
    dx_sums = [dx_parts[0]] + [shift_group(dx_parts[s], -s) for s in range(1, groups)]
    dx_packed = local(sum_pack_kernel, [(ROWS, packed_width)], me, *dx_sums, scalars=1)[0]
    (dx_packed,) = after((dx_packed,), out_back)
    dx_back = exchange(dx_packed)

    own = width // n_rep
    start = (lax.axis_index("rep") * own).astype(jnp.int32)

    def over_reps(value):
        return [value] + [shift_rep(value, s) for s in range(1, n_rep)]

    grad_down = weight_grad(start, over_reps(y_rows), over_reps(hidden), own)
    d_pre, x_rows = after((d_pre, x_rows), dx_packed)
    grad_up = weight_grad(start, over_reps(x_rows), over_reps(d_pre), own)
    (dx_back,) = after((dx_back,), grad_up, grad_down)
    return ffn_out, collect(dx_back, 1), grad_up, grad_down


def solution(mesh):
    placed = (
        P(("lang", "rep"), None),
        P(("lang", "rep"), None),
        P(("lang", "rep")),
        P(("lang", "rep")),
        P(None, "lang"),
        P(None, "lang"),
    )
    return jax.shard_map(
        per_device,
        mesh=mesh,
        in_specs=placed,
        out_specs=(
            P(("lang", "rep"), None),
            P(("lang", "rep"), None),
            P("rep", "lang"),
            P("rep", "lang"),
        ),
        check_vma=False,
    )
```

```python
import functools

import jax
import jax.numpy as jnp
from jax import lax
from jax.experimental import pallas as pl
from jax.experimental.pallas import tpu as pltpu
from jax.sharding import PartitionSpec as P

MODULES = 8
TOK_DEV = 128
CAPACITY = 18
MAIN = 16
SPLIT_COST = 6
VARIANT = "G"
UNPACK_COST = 2
LANES = 128
SPARE = CAPACITY - MAIN
ROWS = MODULES * MAIN
PART = MODULES * CAPACITY

INV_ROOT_TWO = 0.7071067811865476
INV_ROOT_TAU = 0.3989422804014327


def dot(a, b, contract):
    return lax.dot_general(a, b, (contract, ((), ())), preferred_element_type=jnp.float32)


def piece_order():
    place = lax.broadcasted_iota(jnp.int32, (LANES, LANES), 0)
    column = lax.broadcasted_iota(jnp.int32, (LANES, LANES), 1)
    return ((place & 15) * 8 + (place >> 4) == column).astype(jnp.bfloat16)


def spare_rows(cut):
    ordered = dot(piece_order(), cut, ((1,), (0,))).astype(jnp.bfloat16)
    return jnp.concatenate([ordered[16 * p : 16 * (p + 1)] for p in range(8)], axis=1)


def spare_cut(rows):
    ordered = jnp.concatenate([rows[:, LANES * p : LANES * (p + 1)] for p in range(8)], axis=0)
    return dot(piece_order(), ordered, ((0,), (0,))).astype(jnp.bfloat16)


def slot_picks(lang, slot):
    row = lax.broadcasted_iota(jnp.int32, (PART, lang.shape[1]), 0)
    is_main = row < ROWS
    block = jnp.where(is_main, row >> 4, (row - ROWS) >> 1)
    place = jnp.where(is_main, row & 15, MAIN + (row & 1))
    return ((block == lang) & (place == slot)).astype(jnp.bfloat16)


def pack_kernel(me_ref, *refs):
    sources, outs, staged, arrived = refs[:4], refs[4:12], refs[12:16], refs[16]
    copies = [
        pltpu.make_async_copy(source, stage, arrived.at[i])
        for i, (source, stage) in enumerate(zip(sources, staged))
    ]
    for copy in copies:
        copy.start()
    copies[0].wait()
    copies[1].wait()
    picks = slot_picks(staged[0][...] ^ me_ref[0], staged[1][...])
    for array in range(2):
        copies[2 + array].wait()
        width = staged[2].shape[1]
        rows, cut = packed_rows(picks, staged[2 + array][...])
        for z, out_ref in enumerate(outs[4 * array : 4 * (array + 1)]):
            out_ref[:, :width] = rows[32 * z : 32 * (z + 1)]
            out_ref[:, width:] = cut[32 * z : 32 * (z + 1)]


def packed_rows(picks, values):
    rows = dot(picks, values, ((1,), (0,))).astype(jnp.bfloat16)
    return rows[:ROWS], spare_cut(rows[ROWS:])


def split_kernel(*refs):
    messages, outs = refs[:4], refs[4:]
    for z, message_ref in enumerate(messages):
        for place, out_ref in enumerate(outs):
            out_ref[16 * z : 16 * (z + 1)] = message_ref[16 * place : 16 * (place + 1)]


def by_tiles(count):
    tile = min(512, count)
    return [slice(first, first + tile) for first in range(0, count, tile)]


def put_shares(left_ref, right_ref, outs):
    for part in by_tiles(right_ref.shape[0]):
        share = dot(left_ref[...], right_ref[part], ((1,), (1,))).astype(jnp.bfloat16)
        for g, out_ref in enumerate(outs):
            out_ref[:, part] = share[PART * g : PART * (g + 1)]


def forward_kernel(rows_ref, up_ref, down_ref, hidden_ref, slope_ref, *outs):
    for units in by_tiles(up_ref.shape[1]):
        pre = dot(rows_ref[...], up_ref[:, units], ((1,), (0,)))
        share = 0.5 * (1.0 + lax.erf(pre * INV_ROOT_TWO))
        hidden_ref[:, units] = (pre * share).astype(jnp.bfloat16)
        slope_ref[:, units] = share + pre * jnp.exp(-0.5 * pre * pre) * INV_ROOT_TAU
    put_shares(hidden_ref, down_ref, outs)


def backward_kernel(rows_ref, slope_ref, up_ref, down_ref, d_pre_ref, *outs):
    for units in by_tiles(up_ref.shape[1]):
        d_hidden = dot(rows_ref[...], down_ref[:, units], ((1,), (0,)))
        d_pre_ref[:, units] = (d_hidden * slope_ref[:, units]).astype(jnp.bfloat16)
    put_shares(d_pre_ref, up_ref, outs)


NEAR = (0, 2, 4, 6, 1, 3, 5, 7)


def put_rows(packed, rows_ref, first):
    width = rows_ref.shape[1]
    rows_ref[first : first + ROWS] = packed[:, :width]
    rows_ref[first + ROWS : first + PART] = spare_rows(packed[:, width:])


def unpack_near_kernel(groups, *refs):
    for g in range(groups):
        packed = jnp.concatenate([refs[g][...], refs[groups + g][...]], axis=0)
        put_rows(packed, refs[-1], PART * g)


def send_kernel(groups, me_ref, member_ref, *refs):
    packed_ref = refs[-1]
    for i, rows_ref in enumerate(refs[:-1]):
        array, s = divmod(i, groups)
        member = lax.rem(member_ref[0] + groups - s, groups)
        rows = rows_ref[...]
        width = rows.shape[1]
        cut = spare_cut(rows[ROWS:])
        for j, near in enumerate(NEAR):
            device = (me_ref[0] ^ near) * groups + member
            at = pl.ds(pl.multiple_of((device * 2 + array) * MAIN, MAIN), MAIN)
            packed_ref[at, :width] = rows[MAIN * j : MAIN * (j + 1)]
            packed_ref[at, width:] = cut[MAIN * j : MAIN * (j + 1)]


def collect_kernel(groups, lang_ref, slot_ref, packed_ref, *outs):
    picks = slot_picks(lang_ref[...], slot_ref[...])
    for array, values_ref in enumerate(outs):
        width = values_ref.shape[1]
        blocks = []
        for m in range(MODULES):
            total = 0.0
            for g in range(groups):
                first = ((m * groups + g) * 2 + array) * MAIN
                total = total + packed_ref[first : first + MAIN].astype(jnp.float32)
            blocks.append(total.astype(jnp.bfloat16))
        packed = jnp.concatenate(blocks, axis=0)
        rows = jnp.concatenate([packed[:, :width], spare_rows(packed[:, width:])], axis=0)
        values_ref[...] = dot(picks, rows, ((0,), (0,))).astype(jnp.bfloat16)


def weight_grad_kernel(n_parts, start_ref, *refs):
    lefts, rights = refs[:n_parts], refs[n_parts : 2 * n_parts]
    out_ref, turned = refs[2 * n_parts :]
    own, tile = out_ref.shape
    step = pl.program_id(0)

    @pl.when(step == 0)
    def _():
        columns = pl.ds(pl.multiple_of(start_ref[0], LANES), own)
        turned[...] = jnp.concatenate([ref[:, columns] for ref in lefts], axis=0).T

    units = pl.ds(pl.multiple_of(step * tile, LANES), tile)
    right = jnp.concatenate([ref[:, units] for ref in rights], axis=0)
    out_ref[...] = dot(turned[...], right, ((1,), (0,))) * (1.0 / TOK_DEV)


VMEM_SPEC = pl.BlockSpec(memory_space=pltpu.VMEM)
SMEM_SPEC = pl.BlockSpec(memory_space=pltpu.SMEM)


def cost(micros):
    return pl.CostEstimate(flops=int(micros * 1e9), bytes_accessed=0, transcendentals=0)


def shapes_of(shapes):
    return [jax.ShapeDtypeStruct(shape, jnp.bfloat16) for shape in shapes]


def in_hbm(value):
    return pltpu.with_memory_space_constraint(value, pltpu.HBM)


def local(kernel, shapes, *operands, scalars=0, micros=0, grant=4, kept=()):
    outs = [s if isinstance(s, jax.ShapeDtypeStruct) else shapes_of([s])[0] for s in shapes]
    return pl.pallas_call(
        kernel,
        out_shape=[pltpu.VMEM(s.shape, s.dtype) if i in kept else s for i, s in enumerate(outs)],
        in_specs=[SMEM_SPEC] * scalars + [VMEM_SPEC] * (len(operands) - scalars),
        out_specs=[VMEM_SPEC] * len(shapes),
        cost_estimate=cost(micros),
        compiler_params=pltpu.CompilerParams(vmem_limit_bytes=grant << 20),
    )(*operands)


def stage_kernel(*refs):
    sources, outs, arrived = refs[:2], refs[2:4], refs[4]
    copies = [
        pltpu.make_async_copy(source, out, arrived.at[i])
        for i, (source, out) in enumerate(zip(sources, outs))
    ]
    for copy in copies:
        copy.start()
    for copy in copies:
        copy.wait()


def stage(*weights):
    return pl.pallas_call(
        stage_kernel,
        out_shape=[pltpu.VMEM(w.shape, w.dtype) for w in weights],
        in_specs=[pl.BlockSpec(memory_space=pltpu.HBM)] * 2,
        out_specs=[VMEM_SPEC] * 2,
        scratch_shapes=[pltpu.SemaphoreType.DMA((2,))],
        cost_estimate=cost(4),
        compiler_params=pltpu.CompilerParams(vmem_limit_bytes=2 << 20),
    )(*[in_hbm(w) for w in weights])


def pack(me, lang_row, slot_row, tokens, grad_out):
    sources = (lang_row, slot_row, tokens, grad_out)
    packed_width = tokens.shape[1] + LANES
    return pl.pallas_call(
        pack_kernel,
        out_shape=shapes_of([(32, packed_width)] * 8),
        in_specs=[SMEM_SPEC] + [pl.BlockSpec(memory_space=pltpu.HBM)] * 4,
        out_specs=[VMEM_SPEC] * 8,
        scratch_shapes=[pltpu.VMEM(v.shape, v.dtype) for v in sources]
        + [pltpu.SemaphoreType.DMA((4,))],
        cost_estimate=cost(2),
        compiler_params=pltpu.CompilerParams(vmem_limit_bytes=4 << 20),
    )(me, *[in_hbm(v) for v in sources])


def after(values, *earlier):
    return lax.optimization_barrier((*values, *earlier))[: len(values)]


def weight_grad(start, lefts, rights, own):
    n_parts = len(lefts)
    units = rights[0].shape[1]
    depth = sum(left.shape[0] for left in lefts)
    tile = min(512, units)
    if n_parts > 4:
        left = lax.dynamic_slice_in_dim(jnp.concatenate(lefts, axis=0), start, own, axis=1)
        return dot(left, jnp.concatenate(rights, axis=0), ((0,), (0,))) * (1.0 / TOK_DEV)
    return pl.pallas_call(
        functools.partial(weight_grad_kernel, n_parts),
        out_shape=jax.ShapeDtypeStruct((own, units), jnp.float32),
        grid=(units // tile,),
        in_specs=[SMEM_SPEC] + [VMEM_SPEC] * (2 * n_parts),
        out_specs=pl.BlockSpec((own, tile), lambda i: (0, i)),
        scratch_shapes=[pltpu.VMEM((own, depth), jnp.bfloat16)],
        cost_estimate=pl.CostEstimate(
            flops=2 * own * depth * units, bytes_accessed=4 * own * units, transcendentals=0
        ),
        compiler_params=pltpu.CompilerParams(vmem_limit_bytes=12 << 20),
    )(start.reshape(1), *lefts, *rights)


def per_device(tokens, grad_out, lang_ids, slot_ids, w_up, w_down_t):
    n_lang = lax.axis_size("lang")
    n_rep = lax.axis_size("rep")
    groups = n_lang // MODULES
    count, width = tokens.shape
    lang_index = lax.axis_index("lang")
    me = (lang_index // groups).astype(jnp.int32).reshape(1)
    member = lax.rem(lang_index, groups).astype(jnp.int32).reshape(1)
    lang_row, slot_row = lang_ids.reshape(1, count), slot_ids.reshape(1, count)
    packed_width = width + LANES

    def shift_near(value, bits):
        pairs = [
            (m * groups + g, (m ^ bits) * groups + g) for m in range(MODULES) for g in range(groups)
        ]
        return lax.ppermute(value, "lang", pairs)

    def shift_group(value, step):
        pairs = [
            (m * groups + g, m * groups + (g + step) % groups)
            for m in range(MODULES)
            for g in range(groups)
        ]
        return lax.ppermute(value, "lang", pairs)

    def shift_rep(value, step):
        return lax.ppermute(value, "rep", [(r, (r + step) % n_rep) for r in range(n_rep)])

    def over_groups(value):
        return [value] + [shift_group(value, s) for s in range(1, groups)]

    def over_near(blocks, micros):
        got = [blocks[0]] + [shift_near(blocks[z], 2 * z) for z in (1, 2, 3)]
        return local(split_kernel, [(64, packed_width)] * 2, *got, micros=micros)

    def unpack(low, high, micros):
        return unpack_parts(over_groups(low), over_groups(high), micros)

    def unpack_parts(lows, highs, micros):
        return local(
            functools.partial(unpack_near_kernel, groups),
            [(groups * PART, width)],
            *lows,
            *highs,
            micros=micros,
            kept=(0,),
        )[0]

    messages = pack(me, lang_row, slot_row, tokens, grad_out)
    x_low, x_send = over_near(messages[:4], SPLIT_COST)
    y_low, y_send = over_near(messages[4:], 0)
    w_up, w_down_t = stage(w_up, w_down_t)
    x_send, w_up, w_down_t = lax.optimization_barrier((x_send, w_up, w_down_t))
    x_high, y_high = shift_near(x_send, 1), shift_near(y_send, 1)
    if VARIANT == "G":
        (x_high,) = after((x_high,), y_send)
    if VARIANT == "F":
        (x_send2,) = after((x_high,), y_send)
    x_rows = unpack(x_low, x_high, UNPACK_COST)
    y_lows, y_highs = over_groups(y_low), over_groups(y_high)
    if VARIANT == "G":
        (x_rows,) = after((x_rows,), y_high, y_lows[-1])
    y_rows = unpack_parts(y_lows, y_highs, 0)

    depth, units = groups * PART, w_up.shape[1]
    hidden, slope, *out_parts = local(
        forward_kernel,
        shapes_of([(depth, units)])
        + [jax.ShapeDtypeStruct((depth, units), jnp.float32)]
        + shapes_of([(PART, width)] * groups),
        x_rows,
        w_up,
        w_down_t,
        micros=4,
        grant=10,
        kept=(0, 1),
    )
    (y_rows,) = after((y_rows,), *out_parts)
    d_pre, *dx_parts = local(
        backward_kernel,
        [(depth, units)] + [(PART, width)] * groups,
        y_rows,
        slope,
        w_up,
        w_down_t,
        micros=3,
        grant=10,
        kept=(0,),
    )
    own = width // n_rep
    start = (lax.axis_index("rep") * own).astype(jnp.int32)

    def over_reps(value):
        return [value] + [shift_rep(value, s) for s in range(1, n_rep)]

    kernel = functools.partial(send_kernel, groups)
    shape = (n_lang * 2 * MAIN, packed_width)
    packed = local(kernel, [shape], me, member, *out_parts, *dx_parts, scalars=2, micros=1)[0]
    y_rows, hidden, x_rows, d_pre = after((y_rows, hidden, x_rows, d_pre), packed)
    grad_down = weight_grad(start, over_reps(y_rows), over_reps(hidden), own)
    grad_up = weight_grad(start, over_reps(x_rows), over_reps(d_pre), own)
    blocks = packed.reshape(n_lang, 2 * MAIN, packed_width)
    back = lax.all_to_all(blocks, "lang", split_axis=0, concat_axis=0, tiled=True).reshape(shape)
    (back,) = after((back,), grad_down, grad_up)
    kernel = functools.partial(collect_kernel, groups)
    ffn_out, grad_tokens = local(
        kernel, [(count, width)] * 2, lang_row, slot_row, back, micros=1, grant=8
    )
    return ffn_out, grad_tokens, grad_up, grad_down


def solution(mesh):
    placed = (
        P(("lang", "rep"), None),
        P(("lang", "rep"), None),
        P(("lang", "rep")),
        P(("lang", "rep")),
        P(None, "lang"),
        P(None, "lang"),
    )
    return jax.shard_map(
        per_device,
        mesh=mesh,
        in_specs=placed,
        out_specs=(
            P(("lang", "rep"), None),
            P(("lang", "rep"), None),
            P("rep", "lang"),
            P("rep", "lang"),
        ),
        check_vma=False,
    )
```

```python
import functools

import jax
import jax.numpy as jnp
from jax import lax
from jax.experimental import pallas as pl
from jax.experimental.pallas import tpu as pltpu
from jax.sharding import PartitionSpec as P

MODULES = 8
TOK_DEV = 128
CAPACITY = 18
MAIN = 16
SPLIT_COST = 8
VARIANT = "G"
UNPACK_COST = 2
LANES = 128
SPARE = CAPACITY - MAIN
ROWS = MODULES * MAIN
PART = MODULES * CAPACITY

INV_ROOT_TWO = 0.7071067811865476
INV_ROOT_TAU = 0.3989422804014327


def dot(a, b, contract):
    return lax.dot_general(a, b, (contract, ((), ())), preferred_element_type=jnp.float32)


def piece_order(pieces):
    place = lax.broadcasted_iota(jnp.int32, (16 * pieces, LANES), 0)
    column = lax.broadcasted_iota(jnp.int32, (16 * pieces, LANES), 1)
    piece, row = place >> 4, place & 15
    return (((row >> 1) * 16 + (row & 1) * pieces + piece) == column).astype(jnp.bfloat16)


def spare_rows(cut, pieces):
    ordered = dot(piece_order(pieces), cut, ((1,), (0,))).astype(jnp.bfloat16)
    return jnp.concatenate([ordered[16 * p : 16 * (p + 1)] for p in range(pieces)], axis=1)


def spare_cut(rows):
    pieces = rows.shape[1] // LANES
    ordered = [rows[:, LANES * p : LANES * (p + 1)] for p in range(pieces)]
    ordered = jnp.concatenate(ordered, axis=0)
    return dot(piece_order(pieces), ordered, ((0,), (0,))).astype(jnp.bfloat16)


def slot_picks(lang, slot):
    row = lax.broadcasted_iota(jnp.int32, (PART, lang.shape[1]), 0)
    is_main = row < ROWS
    block = jnp.where(is_main, row >> 4, (row - ROWS) >> 1)
    place = jnp.where(is_main, row & 15, MAIN + (row & 1))
    return ((block == lang) & (place == slot)).astype(jnp.bfloat16)


def pack_kernel(me_ref, *refs):
    sources, outs, staged, arrived = refs[:4], refs[4:12], refs[12:16], refs[16]
    copies = [
        pltpu.make_async_copy(source, stage, arrived.at[i])
        for i, (source, stage) in enumerate(zip(sources, staged))
    ]
    for copy in copies:
        copy.start()
    copies[0].wait()
    copies[1].wait()
    picks = slot_picks(staged[0][...] ^ me_ref[0], staged[1][...])
    for array in range(2):
        copies[2 + array].wait()
        width = staged[2].shape[1]
        rows, cut = packed_rows(picks, staged[2 + array][...])
        for z, out_ref in enumerate(outs[4 * array : 4 * (array + 1)]):
            out_ref[:, :width] = rows[32 * z : 32 * (z + 1)]
            out_ref[:, width:] = cut[32 * z : 32 * (z + 1)]


def packed_rows(picks, values):
    rows = dot(picks, values, ((1,), (0,))).astype(jnp.bfloat16)
    return rows[:ROWS], spare_cut(rows[ROWS:])


def split_kernel(*refs):
    messages, outs = refs[:4], refs[4:]
    for z, message_ref in enumerate(messages):
        for place, out_ref in enumerate(outs):
            out_ref[16 * z : 16 * (z + 1)] = message_ref[16 * place : 16 * (place + 1)]


def by_tiles(count):
    tile = min(512, count)
    return [slice(first, first + tile) for first in range(0, count, tile)]


def forward_kernel(groups, member_ref, rows_ref, up_ref, down_ref, hidden_ref, slope_ref, *outs):
    for units in by_tiles(up_ref.shape[1]):
        pre = dot(rows_ref[...], up_ref[:, units], ((1,), (0,)))
        share = 0.5 * (1.0 + lax.erf(pre * INV_ROOT_TWO))
        hidden_ref[:, units] = (pre * share).astype(jnp.bfloat16)
        slope_ref[:, units] = share + pre * jnp.exp(-0.5 * pre * pre) * INV_ROOT_TAU
    for s, out_ref in enumerate(outs):
        width = out_ref.shape[1]
        first = pl.multiple_of(lax.rem(member_ref[0] + s, groups) * width, LANES)
        weights = down_ref[pl.ds(first, width)]
        out_ref[...] = dot(hidden_ref[...], weights, ((1,), (1,))).astype(jnp.bfloat16)


def backward_kernel(rows_ref, slope_ref, up_ref, down_ref, d_pre_ref, *outs):
    for units in by_tiles(up_ref.shape[1]):
        d_hidden = dot(rows_ref[...], down_ref[:, units], ((1,), (0,)))
        d_pre_ref[:, units] = (d_hidden * slope_ref[:, units]).astype(jnp.bfloat16)
    for part in by_tiles(up_ref.shape[0]):
        share = dot(d_pre_ref[...], up_ref[part], ((1,), (1,))).astype(jnp.bfloat16)
        for g, out_ref in enumerate(outs):
            out_ref[:, part] = share[PART * g : PART * (g + 1)]


NEAR = (0, 2, 4, 6, 1, 3, 5, 7)


def put_rows(packed, rows_ref, first):
    width = rows_ref.shape[1]
    rows_ref[first : first + ROWS] = packed[:, :width]
    rows_ref[first + ROWS : first + PART] = spare_rows(packed[:, width:], width // LANES)


def unpack_near_kernel(groups, *refs):
    for g in range(groups):
        packed = jnp.concatenate([refs[g][...], refs[groups + g][...]], axis=0)
        put_rows(packed, refs[-1], PART * g)


def send_kernel(groups, me_ref, member_ref, *refs):
    sums, dx_refs, packed_ref = refs[:groups], refs[groups:-1], refs[-1]
    for s in range(groups):
        member = lax.rem(member_ref[0] + groups - s, groups)
        total = 0.0
        for t in range(groups):
            part = PART * ((s - t) % groups)
            total = total + sums[t][part : part + PART].astype(jnp.float32)
        first = 0
        for rows in (dx_refs[s][...], total.astype(jnp.bfloat16)):
            width = rows.shape[1]
            cut = spare_cut(rows[ROWS:])
            for j, near in enumerate(NEAR):
                device = (me_ref[0] ^ near) * groups + member
                at = pl.ds(pl.multiple_of(device * MAIN, MAIN), MAIN)
                main = slice(MAIN * j, MAIN * (j + 1))
                packed_ref[at, first : first + width] = rows[main]
                packed_ref[at, first + width : first + width + LANES] = cut[main]
            first += width + LANES


def collect_kernel(groups, lang_ref, slot_ref, packed_ref, out_ref, dx_ref):
    picks = slot_picks(lang_ref[...], slot_ref[...]).T
    width = dx_ref.shape[1]
    share = width // groups
    middle = width + LANES

    def blocks(g, columns):
        firsts = [MAIN * (m * groups + g) for m in range(MODULES)]
        return jnp.concatenate([packed_ref[f : f + MAIN, columns] for f in firsts], axis=0)

    def pick(main, cut):
        rows = jnp.concatenate([main, spare_rows(cut, main.shape[1] // LANES)], axis=0)
        return dot(picks, rows, ((1,), (0,))).astype(jnp.bfloat16)

    total = 0.0
    for g in range(groups):
        total = total + blocks(g, slice(0, middle)).astype(jnp.float32)
        main = blocks(g, slice(middle, middle + share))
        cut = blocks(g, slice(middle + share, middle + share + LANES))
        out_ref[:, share * g : share * (g + 1)] = pick(main, cut)
    total = total.astype(jnp.bfloat16)
    dx_ref[...] = pick(total[:, :width], total[:, width:])


def weight_grad_kernel(n_parts, start_ref, *refs):
    lefts, rights = refs[:n_parts], refs[n_parts : 2 * n_parts]
    out_ref, turned = refs[2 * n_parts :]
    own, tile = out_ref.shape
    step = pl.program_id(0)

    @pl.when(step == 0)
    def _():
        columns = pl.ds(pl.multiple_of(start_ref[0], LANES), own)
        turned[...] = jnp.concatenate([ref[:, columns] for ref in lefts], axis=0).T

    units = pl.ds(pl.multiple_of(step * tile, LANES), tile)
    right = jnp.concatenate([ref[:, units] for ref in rights], axis=0)
    out_ref[...] = dot(turned[...], right, ((1,), (0,))) * (1.0 / TOK_DEV)


VMEM_SPEC = pl.BlockSpec(memory_space=pltpu.VMEM)
SMEM_SPEC = pl.BlockSpec(memory_space=pltpu.SMEM)


def cost(micros):
    return pl.CostEstimate(flops=int(micros * 1e9), bytes_accessed=0, transcendentals=0)


def shapes_of(shapes):
    return [jax.ShapeDtypeStruct(shape, jnp.bfloat16) for shape in shapes]


def in_hbm(value):
    return pltpu.with_memory_space_constraint(value, pltpu.HBM)


def local(kernel, shapes, *operands, scalars=0, micros=0, grant=4, kept=()):
    outs = [s if isinstance(s, jax.ShapeDtypeStruct) else shapes_of([s])[0] for s in shapes]
    return pl.pallas_call(
        kernel,
        out_shape=[pltpu.VMEM(s.shape, s.dtype) if i in kept else s for i, s in enumerate(outs)],
        in_specs=[SMEM_SPEC] * scalars + [VMEM_SPEC] * (len(operands) - scalars),
        out_specs=[VMEM_SPEC] * len(shapes),
        cost_estimate=cost(micros),
        compiler_params=pltpu.CompilerParams(vmem_limit_bytes=grant << 20),
    )(*operands)


def stage_kernel(*refs):
    sources, outs, arrived = refs[:2], refs[2:4], refs[4]
    copies = [
        pltpu.make_async_copy(source, out, arrived.at[i])
        for i, (source, out) in enumerate(zip(sources, outs))
    ]
    for copy in copies:
        copy.start()
    for copy in copies:
        copy.wait()


def stage(*weights):
    return pl.pallas_call(
        stage_kernel,
        out_shape=[pltpu.VMEM(w.shape, w.dtype) for w in weights],
        in_specs=[pl.BlockSpec(memory_space=pltpu.HBM)] * 2,
        out_specs=[VMEM_SPEC] * 2,
        scratch_shapes=[pltpu.SemaphoreType.DMA((2,))],
        cost_estimate=cost(4),
        compiler_params=pltpu.CompilerParams(vmem_limit_bytes=2 << 20),
    )(*[in_hbm(w) for w in weights])


def pack(me, lang_row, slot_row, tokens, grad_out):
    sources = (lang_row, slot_row, tokens, grad_out)
    packed_width = tokens.shape[1] + LANES
    return pl.pallas_call(
        pack_kernel,
        out_shape=shapes_of([(32, packed_width)] * 8),
        in_specs=[SMEM_SPEC] + [pl.BlockSpec(memory_space=pltpu.HBM)] * 4,
        out_specs=[VMEM_SPEC] * 8,
        scratch_shapes=[pltpu.VMEM(v.shape, v.dtype) for v in sources]
        + [pltpu.SemaphoreType.DMA((4,))],
        cost_estimate=cost(2),
        compiler_params=pltpu.CompilerParams(vmem_limit_bytes=4 << 20),
    )(me, *[in_hbm(v) for v in sources])


def after(values, *earlier):
    return lax.optimization_barrier((*values, *earlier))[: len(values)]


def weight_grad(start, lefts, rights, own):
    n_parts = len(lefts)
    units = rights[0].shape[1]
    depth = sum(left.shape[0] for left in lefts)
    tile = min(512, units)
    if n_parts > 4:
        left = lax.dynamic_slice_in_dim(jnp.concatenate(lefts, axis=0), start, own, axis=1)
        return dot(left, jnp.concatenate(rights, axis=0), ((0,), (0,))) * (1.0 / TOK_DEV)
    return pl.pallas_call(
        functools.partial(weight_grad_kernel, n_parts),
        out_shape=jax.ShapeDtypeStruct((own, units), jnp.float32),
        grid=(units // tile,),
        in_specs=[SMEM_SPEC] + [VMEM_SPEC] * (2 * n_parts),
        out_specs=pl.BlockSpec((own, tile), lambda i: (0, i)),
        scratch_shapes=[pltpu.VMEM((own, depth), jnp.bfloat16)],
        cost_estimate=pl.CostEstimate(
            flops=2 * own * depth * units, bytes_accessed=4 * own * units, transcendentals=0
        ),
        compiler_params=pltpu.CompilerParams(vmem_limit_bytes=12 << 20),
    )(start.reshape(1), *lefts, *rights)


def per_device(tokens, grad_out, lang_ids, slot_ids, w_up, w_down_t):
    n_lang = lax.axis_size("lang")
    n_rep = lax.axis_size("rep")
    groups = n_lang // MODULES
    count, width = tokens.shape
    lang_index = lax.axis_index("lang")
    me = (lang_index // groups).astype(jnp.int32).reshape(1)
    member = lax.rem(lang_index, groups).astype(jnp.int32).reshape(1)
    lang_row, slot_row = lang_ids.reshape(1, count), slot_ids.reshape(1, count)
    packed_width = width + LANES

    def shift_near(value, bits):
        pairs = [
            (m * groups + g, (m ^ bits) * groups + g) for m in range(MODULES) for g in range(groups)
        ]
        return lax.ppermute(value, "lang", pairs)

    def shift_group(value, step):
        pairs = [
            (m * groups + g, m * groups + (g + step) % groups)
            for m in range(MODULES)
            for g in range(groups)
        ]
        return lax.ppermute(value, "lang", pairs)

    def shift_rep(value, step):
        return lax.ppermute(value, "rep", [(r, (r + step) % n_rep) for r in range(n_rep)])

    def over_groups(value):
        return [value] + [shift_group(value, s) for s in range(1, groups)]

    def over_near(blocks, micros):
        got = [blocks[0]] + [shift_near(blocks[z], 2 * z) for z in (1, 2, 3)]
        return local(split_kernel, [(64, packed_width)] * 2, *got, micros=micros)

    def unpack(low, high, micros):
        return unpack_parts(over_groups(low), over_groups(high), micros)

    def unpack_parts(lows, highs, micros):
        return local(
            functools.partial(unpack_near_kernel, groups),
            [(groups * PART, width)],
            *lows,
            *highs,
            micros=micros,
            kept=(0,),
        )[0]

    messages = pack(me, lang_row, slot_row, tokens, grad_out)
    x_low, x_send = over_near(messages[:4], 0)
    y_low, y_send = over_near(messages[4:], SPLIT_COST)
    w_up, w_down_t = stage(w_up, w_down_t)
    (x_send,) = after((x_send,), w_up)
    x_high, y_high = shift_near(x_send, 1), shift_near(y_send, 1)
    x_lows = over_groups(x_low)
    (x_high,) = after((x_high,), y_send, x_lows[-1])
    x_rows = unpack_parts(x_lows, over_groups(x_high), UNPACK_COST)
    y_lows, y_highs = over_groups(y_low), over_groups(y_high)
    (x_rows,) = after((x_rows,), y_high)
    y_rows = unpack_parts(y_lows, y_highs, 0)

    depth, units = groups * PART, w_up.shape[1]
    hidden, slope, *out_parts = local(
        functools.partial(forward_kernel, groups),
        shapes_of([(depth, units)])
        + [jax.ShapeDtypeStruct((depth, units), jnp.float32)]
        + shapes_of([(depth, width // groups)] * groups),
        member,
        x_rows,
        w_up,
        w_down_t,
        scalars=1,
        micros=4,
        grant=10,
        kept=(0, 1),
    )
    (y_rows,) = after((y_rows,), *out_parts)
    d_pre, *dx_parts = local(
        backward_kernel,
        [(depth, units)] + [(PART, width)] * groups,
        y_rows,
        slope,
        w_up,
        w_down_t,
        micros=3,
        grant=10,
        kept=(0,),
    )
    own = width // n_rep
    start = (lax.axis_index("rep") * own).astype(jnp.int32)

    def over_reps(value):
        return [value] + [shift_rep(value, s) for s in range(1, n_rep)]

    sums = [out_parts[0]] + [shift_group(out_parts[s], s) for s in range(1, groups)]
    kernel = functools.partial(send_kernel, groups)
    shape = (n_lang * MAIN, packed_width + width // groups + LANES)
    packed = local(kernel, [shape], me, member, *sums, *dx_parts, scalars=2, micros=1)[0]
    y_rows, hidden, x_rows, d_pre = after((y_rows, hidden, x_rows, d_pre), packed)
    grad_down = weight_grad(start, over_reps(y_rows), over_reps(hidden), own)
    grad_up = weight_grad(start, over_reps(x_rows), over_reps(d_pre), own)
    blocks = packed.reshape(n_lang, MAIN, shape[1])
    back = lax.all_to_all(blocks, "lang", split_axis=0, concat_axis=0, tiled=True).reshape(shape)
    (back,) = after((back,), grad_down, grad_up)
    kernel = functools.partial(collect_kernel, groups)
    ffn_out, grad_tokens = local(
        kernel, [(count, width)] * 2, lang_row, slot_row, back, micros=1, grant=8
    )
    return ffn_out, grad_tokens, grad_up, grad_down


def solution(mesh):
    placed = (
        P(("lang", "rep"), None),
        P(("lang", "rep"), None),
        P(("lang", "rep")),
        P(("lang", "rep")),
        P(None, "lang"),
        P(None, "lang"),
    )
    return jax.shard_map(
        per_device,
        mesh=mesh,
        in_specs=placed,
        out_specs=(
            P(("lang", "rep"), None),
            P(("lang", "rep"), None),
            P("rep", "lang"),
            P("rep", "lang"),
        ),
        check_vma=False,
    )
```

```python
import functools

import jax
import jax.numpy as jnp
from jax import lax
from jax.experimental import pallas as pl
from jax.experimental.pallas import tpu as pltpu
from jax.sharding import PartitionSpec as P

MODULES = 8
TOK_DEV = 128
CAPACITY = 18
MAIN = 16
SPLIT_COST = 8
FORWARD_COST = 4
VARIANT = "G"
UNPACK_COST = 2
LANES = 128
SPARE = CAPACITY - MAIN
ROWS = MODULES * MAIN
PART = MODULES * CAPACITY

INV_ROOT_TWO = 0.7071067811865476
INV_ROOT_TAU = 0.3989422804014327


def dot(a, b, contract):
    return lax.dot_general(a, b, (contract, ((), ())), preferred_element_type=jnp.float32)


def piece_order(pieces):
    place = lax.broadcasted_iota(jnp.int32, (16 * pieces, LANES), 0)
    column = lax.broadcasted_iota(jnp.int32, (16 * pieces, LANES), 1)
    piece, row = place >> 4, place & 15
    return (((row >> 1) * 16 + (row & 1) * pieces + piece) == column).astype(jnp.bfloat16)


def spare_rows(cut, pieces):
    ordered = dot(piece_order(pieces), cut, ((1,), (0,))).astype(jnp.bfloat16)
    return jnp.concatenate([ordered[16 * p : 16 * (p + 1)] for p in range(pieces)], axis=1)


def spare_cut(rows):
    pieces = rows.shape[1] // LANES
    ordered = [rows[:, LANES * p : LANES * (p + 1)] for p in range(pieces)]
    ordered = jnp.concatenate(ordered, axis=0)
    return dot(piece_order(pieces), ordered, ((0,), (0,))).astype(jnp.bfloat16)


def slot_picks(lang, slot):
    row = lax.broadcasted_iota(jnp.int32, (PART, lang.shape[1]), 0)
    is_main = row < ROWS
    block = jnp.where(is_main, row >> 4, (row - ROWS) >> 1)
    place = jnp.where(is_main, row & 15, MAIN + (row & 1))
    return ((block == lang) & (place == slot)).astype(jnp.bfloat16)


def pack_kernel(me_ref, *refs):
    sources, outs, staged, arrived = refs[:3], refs[3:7], refs[7:10], refs[10]
    copies = [
        pltpu.make_async_copy(source, stage, arrived.at[i])
        for i, (source, stage) in enumerate(zip(sources, staged))
    ]
    for copy in copies:
        copy.start()
    for copy in copies:
        copy.wait()
    width = staged[2].shape[1]
    picks = slot_picks(staged[0][...] ^ me_ref[0], staged[1][...])
    rows, cut = packed_rows(picks, staged[2][...])
    for z, out_ref in enumerate(outs):
        out_ref[:, :width] = rows[32 * z : 32 * (z + 1)]
        out_ref[:, width:] = cut[32 * z : 32 * (z + 1)]


def packed_rows(picks, values):
    rows = dot(picks, values, ((1,), (0,))).astype(jnp.bfloat16)
    return rows[:ROWS], spare_cut(rows[ROWS:])


def split_kernel(*refs):
    messages, outs = refs[:4], refs[4:]
    for z, message_ref in enumerate(messages):
        for place, out_ref in enumerate(outs):
            out_ref[16 * z : 16 * (z + 1)] = message_ref[16 * place : 16 * (place + 1)]


def by_tiles(count):
    tile = min(512, count)
    return [slice(first, first + tile) for first in range(0, count, tile)]


def forward_kernel(groups, member_ref, rows_ref, up_hbm, down_hbm, *refs):
    hidden_ref, slope_ref, up_ref, down_ref = refs[:4]
    outs, arrived = refs[4:-1], refs[-1]
    tiles, width = by_tiles(up_ref.shape[1]), outs[0].shape[1]
    bands = [slice(first, first + width) for first in range(0, down_ref.shape[0], width)]
    pairs = [(up_hbm.at[:, units], up_ref.at[:, units]) for units in tiles]
    pairs += [(down_hbm.at[band], down_ref.at[band]) for band in bands]
    copies = [pltpu.make_async_copy(*pair, arrived.at[i]) for i, pair in enumerate(pairs)]
    for copy in copies:
        copy.start()
    for units, copy in zip(tiles, copies):
        copy.wait()
        pre = dot(rows_ref[...], up_ref[:, units], ((1,), (0,)))
        share = 0.5 * (1.0 + lax.erf(pre * INV_ROOT_TWO))
        hidden_ref[:, units] = (pre * share).astype(jnp.bfloat16)
        slope_ref[:, units] = share + pre * jnp.exp(-0.5 * pre * pre) * INV_ROOT_TAU
    for copy in copies[len(tiles) :]:
        copy.wait()
    for s, out_ref in enumerate(outs):
        first = pl.multiple_of(lax.rem(member_ref[0] + s, groups) * width, LANES)
        weights = down_ref[pl.ds(first, width)]
        out_ref[...] = dot(hidden_ref[...], weights, ((1,), (1,))).astype(jnp.bfloat16)


def forward(groups, member, x_rows, w_up, w_down_t):
    depth, (width, units) = x_rows.shape[0], w_up.shape
    return pl.pallas_call(
        functools.partial(forward_kernel, groups),
        out_shape=[
            pltpu.VMEM((depth, units), jnp.bfloat16),
            pltpu.VMEM((depth, units), jnp.float32),
            pltpu.VMEM(w_up.shape, w_up.dtype),
            pltpu.VMEM(w_down_t.shape, w_down_t.dtype),
        ]
        + shapes_of([(depth, width // groups)] * groups),
        in_specs=[SMEM_SPEC, VMEM_SPEC] + [pl.BlockSpec(memory_space=pltpu.HBM)] * 2,
        out_specs=[VMEM_SPEC] * (4 + groups),
        scratch_shapes=[pltpu.SemaphoreType.DMA((len(by_tiles(units)) + groups,))],
        cost_estimate=cost(FORWARD_COST),
        compiler_params=pltpu.CompilerParams(vmem_limit_bytes=10 << 20),
    )(member, x_rows, in_hbm(w_up), in_hbm(w_down_t))


def backward_kernel(rows_ref, slope_ref, up_ref, down_ref, d_pre_ref, *outs):
    for units in by_tiles(up_ref.shape[1]):
        d_hidden = dot(rows_ref[...], down_ref[:, units], ((1,), (0,)))
        d_pre_ref[:, units] = (d_hidden * slope_ref[:, units]).astype(jnp.bfloat16)
    for part in by_tiles(up_ref.shape[0]):
        share = dot(d_pre_ref[...], up_ref[part], ((1,), (1,))).astype(jnp.bfloat16)
        for g, out_ref in enumerate(outs):
            out_ref[:, part] = share[PART * g : PART * (g + 1)]


NEAR = (0, 2, 4, 6, 1, 3, 5, 7)


def put_rows(packed, rows_ref, first):
    width = rows_ref.shape[1]
    rows_ref[first : first + ROWS] = packed[:, :width]
    rows_ref[first + ROWS : first + PART] = spare_rows(packed[:, width:], width // LANES)


def unpack_near_kernel(groups, *refs):
    for g in range(groups):
        packed = jnp.concatenate([refs[g][...], refs[groups + g][...]], axis=0)
        put_rows(packed, refs[-1], PART * g)


def send_kernel(groups, me_ref, member_ref, *refs):
    sums, dx_refs, packed_ref = refs[:groups], refs[groups:-1], refs[-1]
    for s in range(groups):
        member = lax.rem(member_ref[0] + groups - s, groups)
        total = 0.0
        for t in range(groups):
            part = PART * ((s - t) % groups)
            total = total + sums[t][part : part + PART].astype(jnp.float32)
        first = 0
        for rows in (dx_refs[s][...], total.astype(jnp.bfloat16)):
            width = rows.shape[1]
            cut = spare_cut(rows[ROWS:])
            for j, near in enumerate(NEAR):
                device = (me_ref[0] ^ near) * groups + member
                at = pl.ds(pl.multiple_of(device * MAIN, MAIN), MAIN)
                main = slice(MAIN * j, MAIN * (j + 1))
                packed_ref[at, first : first + width] = rows[main]
                packed_ref[at, first + width : first + width + LANES] = cut[main]
            first += width + LANES


def collect_kernel(groups, lang_ref, slot_ref, packed_ref, out_ref, dx_ref):
    picks = slot_picks(lang_ref[...], slot_ref[...]).T
    width = dx_ref.shape[1]
    share = width // groups
    middle = width + LANES

    def blocks(g, columns):
        firsts = [MAIN * (m * groups + g) for m in range(MODULES)]
        return jnp.concatenate([packed_ref[f : f + MAIN, columns] for f in firsts], axis=0)

    def pick(main, cut):
        rows = jnp.concatenate([main, spare_rows(cut, main.shape[1] // LANES)], axis=0)
        return dot(picks, rows, ((1,), (0,))).astype(jnp.bfloat16)

    total = 0.0
    for g in range(groups):
        total = total + blocks(g, slice(0, middle)).astype(jnp.float32)
        main = blocks(g, slice(middle, middle + share))
        cut = blocks(g, slice(middle + share, middle + share + LANES))
        out_ref[:, share * g : share * (g + 1)] = pick(main, cut)
    total = total.astype(jnp.bfloat16)
    dx_ref[...] = pick(total[:, :width], total[:, width:])


def weight_grads_kernel(n_parts, start_ref, *refs):
    operands, outs, turned = refs[: 4 * n_parts], refs[4 * n_parts : -1], refs[-1]
    own, tile = outs[0].shape
    tiles = pl.num_programs(0) // 2

    for i, out_ref in enumerate(outs):
        lefts = operands[2 * n_parts * i : 2 * n_parts * i + n_parts]
        rights = operands[2 * n_parts * i + n_parts : 2 * n_parts * (i + 1)]

        @pl.when(pl.program_id(0) == i * tiles)
        def _(lefts=lefts):
            columns = pl.ds(pl.multiple_of(start_ref[0], LANES), own)
            turned[...] = jnp.concatenate([ref[:, columns] for ref in lefts], axis=0).T

        @pl.when(pl.program_id(0) // tiles == i)
        def _(i=i, rights=rights, out_ref=out_ref):
            first = (pl.program_id(0) - i * tiles) * tile
            units = pl.ds(pl.multiple_of(first, LANES), tile)
            right = jnp.concatenate([ref[:, units] for ref in rights], axis=0)
            out_ref[...] = dot(turned[...], right, ((1,), (0,))) * (1.0 / TOK_DEV)


VMEM_SPEC = pl.BlockSpec(memory_space=pltpu.VMEM)
SMEM_SPEC = pl.BlockSpec(memory_space=pltpu.SMEM)


def cost(micros):
    return pl.CostEstimate(flops=int(micros * 1e9), bytes_accessed=0, transcendentals=0)


def shapes_of(shapes):
    return [jax.ShapeDtypeStruct(shape, jnp.bfloat16) for shape in shapes]


def in_hbm(value):
    return pltpu.with_memory_space_constraint(value, pltpu.HBM)


def local(kernel, shapes, *operands, scalars=0, micros=0, grant=4, kept=()):
    outs = [s if isinstance(s, jax.ShapeDtypeStruct) else shapes_of([s])[0] for s in shapes]
    return pl.pallas_call(
        kernel,
        out_shape=[pltpu.VMEM(s.shape, s.dtype) if i in kept else s for i, s in enumerate(outs)],
        in_specs=[SMEM_SPEC] * scalars + [VMEM_SPEC] * (len(operands) - scalars),
        out_specs=[VMEM_SPEC] * len(shapes),
        cost_estimate=cost(micros),
        compiler_params=pltpu.CompilerParams(vmem_limit_bytes=grant << 20),
    )(*operands)


def pack(me, *sources):
    packed_width = sources[2].shape[1] + LANES
    return pl.pallas_call(
        pack_kernel,
        out_shape=shapes_of([(32, packed_width)] * 4),
        in_specs=[SMEM_SPEC] + [pl.BlockSpec(memory_space=pltpu.HBM)] * 3,
        out_specs=[VMEM_SPEC] * 4,
        scratch_shapes=[pltpu.VMEM(v.shape, v.dtype) for v in sources]
        + [pltpu.SemaphoreType.DMA((3,))],
        cost_estimate=cost(2),
        compiler_params=pltpu.CompilerParams(vmem_limit_bytes=4 << 20),
    )(me, *[in_hbm(v) for v in sources])


def after(values, *earlier):
    return lax.optimization_barrier((*values, *earlier))[: len(values)]


def weight_grads(start, pairs, own):
    n_parts, units = len(pairs[0][0]), pairs[0][1][0].shape[1]
    depth = sum(left.shape[0] for left in pairs[0][0])
    tile = min(512, units)
    tiles = units // tile
    if n_parts > 4:
        grads = []
        for lefts, rights in pairs:
            left = lax.dynamic_slice_in_dim(jnp.concatenate(lefts, axis=0), start, own, axis=1)
            right = jnp.concatenate(rights, axis=0)
            grads.append(dot(left, right, ((0,), (0,))) * (1.0 / TOK_DEV))
        return grads
    operands = [v for lefts, rights in pairs for v in (*lefts, *rights)]
    return pl.pallas_call(
        functools.partial(weight_grads_kernel, n_parts),
        out_shape=[jax.ShapeDtypeStruct((own, units), jnp.float32)] * 2,
        grid=(2 * tiles,),
        in_specs=[SMEM_SPEC] + [VMEM_SPEC] * len(operands),
        out_specs=[
            pl.BlockSpec((own, tile), lambda i: (0, jnp.minimum(i, tiles - 1))),
            pl.BlockSpec((own, tile), lambda i: (0, jnp.maximum(i - tiles, 0))),
        ],
        scratch_shapes=[pltpu.VMEM((own, depth), jnp.bfloat16)],
        cost_estimate=cost(4),
        compiler_params=pltpu.CompilerParams(vmem_limit_bytes=24 << 20),
    )(start.reshape(1), *operands[: 3 * n_parts], *[in_hbm(v) for v in operands[3 * n_parts :]])


def per_device(tokens, grad_out, lang_ids, slot_ids, w_up, w_down_t):
    n_lang = lax.axis_size("lang")
    n_rep = lax.axis_size("rep")
    groups = n_lang // MODULES
    count, width = tokens.shape
    lang_index = lax.axis_index("lang")
    me = (lang_index // groups).astype(jnp.int32).reshape(1)
    member = lax.rem(lang_index, groups).astype(jnp.int32).reshape(1)
    lang_row, slot_row = lang_ids.reshape(1, count), slot_ids.reshape(1, count)
    packed_width = width + LANES

    def shift_near(value, bits):
        pairs = [
            (m * groups + g, (m ^ bits) * groups + g) for m in range(MODULES) for g in range(groups)
        ]
        return lax.ppermute(value, "lang", pairs)

    def shift_group(value, step):
        pairs = [
            (m * groups + g, m * groups + (g + step) % groups)
            for m in range(MODULES)
            for g in range(groups)
        ]
        return lax.ppermute(value, "lang", pairs)

    def shift_rep(value, step):
        return lax.ppermute(value, "rep", [(r, (r + step) % n_rep) for r in range(n_rep)])

    def over_groups(value):
        return [value] + [shift_group(value, s) for s in range(1, groups)]

    def over_near(blocks, micros):
        got = [blocks[0]] + [shift_near(blocks[z], 2 * z) for z in (1, 2, 3)]
        return local(split_kernel, [(64, packed_width)] * 2, *got, micros=micros)

    def unpack(low, high, micros):
        return unpack_parts(over_groups(low), over_groups(high), micros)

    def unpack_parts(lows, highs, micros):
        return local(
            functools.partial(unpack_near_kernel, groups),
            [(groups * PART, width)],
            *lows,
            *highs,
            micros=micros,
            kept=(0,),
        )[0]

    messages = pack(me, lang_row, slot_row, tokens) + pack(me, lang_row, slot_row, grad_out)
    x_low, x_send = over_near(messages[:4], 0)
    y_low, y_send = over_near(messages[4:], SPLIT_COST)
    x_high, y_high = shift_near(x_send, 1), shift_near(y_send, 1)
    x_lows = over_groups(x_low)
    (x_high,) = after((x_high,), y_send, x_lows[-1])
    x_rows = unpack_parts(x_lows, over_groups(x_high), UNPACK_COST)
    y_lows, y_highs = over_groups(y_low), over_groups(y_high)
    (x_rows,) = after((x_rows,), y_high)
    y_rows = unpack_parts(y_lows, y_highs, 0)

    depth, units = groups * PART, w_up.shape[1]
    hidden, slope, w_up, w_down_t, *out_parts = forward(groups, member, x_rows, w_up, w_down_t)
    (y_rows,) = after((y_rows,), *out_parts)
    d_pre, *dx_parts = local(
        backward_kernel,
        [(depth, units)] + [(PART, width)] * groups,
        y_rows,
        slope,
        w_up,
        w_down_t,
        micros=3,
        grant=10,
        kept=(0,),
    )
    own = width // n_rep
    start = (lax.axis_index("rep") * own).astype(jnp.int32)

    def over_reps(value):
        return [value] + [shift_rep(value, s) for s in range(1, n_rep)]

    sums = [out_parts[0]] + [shift_group(out_parts[s], s) for s in range(1, groups)]
    kernel = functools.partial(send_kernel, groups)
    shape = (n_lang * MAIN, packed_width + width // groups + LANES)
    packed = local(kernel, [shape], me, member, *sums, *dx_parts, scalars=2, micros=1)[0]
    y_rows, hidden, x_rows, d_pre = after((y_rows, hidden, x_rows, d_pre), packed)
    pairs = [
        (over_reps(y_rows), over_reps(hidden)),
        (over_reps(x_rows), over_reps(d_pre)),
    ]
    grad_down, grad_up = weight_grads(start, pairs, own)
    blocks = packed.reshape(n_lang, MAIN, shape[1])
    back = lax.all_to_all(blocks, "lang", split_axis=0, concat_axis=0, tiled=True).reshape(shape)
    (back,) = after((back,), grad_down, grad_up)
    kernel = functools.partial(collect_kernel, groups)
    ffn_out, grad_tokens = local(
        kernel, [(count, width)] * 2, lang_row, slot_row, back, micros=1, grant=8
    )
    return ffn_out, grad_tokens, grad_up, grad_down


def solution(mesh):
    placed = (
        P(("lang", "rep"), None),
        P(("lang", "rep"), None),
        P(("lang", "rep")),
        P(("lang", "rep")),
        P(None, "lang"),
        P(None, "lang"),
    )
    return jax.shard_map(
        per_device,
        mesh=mesh,
        in_specs=placed,
        out_specs=(
            P(("lang", "rep"), None),
            P(("lang", "rep"), None),
            P("rep", "lang"),
            P("rep", "lang"),
        ),
        check_vma=False,
    )
```

```python
import functools

import jax
import jax.numpy as jnp
from jax import lax
from jax.experimental import pallas as pl
from jax.experimental.pallas import tpu as pltpu
from jax.sharding import PartitionSpec as P

MODULES = 8
TOK_DEV = 128
CAPACITY = 18
MAIN = 16
SPLIT_COST = 8
FORWARD_COST = 4
VARIANT = "G"
UNPACK_COST = 2
LANES = 128
SPARE = CAPACITY - MAIN
ROWS = MODULES * MAIN
PART = MODULES * CAPACITY

INV_ROOT_TWO = 0.7071067811865476
INV_ROOT_TAU = 0.3989422804014327


def dot(a, b, contract):
    return lax.dot_general(a, b, (contract, ((), ())), preferred_element_type=jnp.float32)


def piece_order(pieces):
    place = lax.broadcasted_iota(jnp.int32, (16 * pieces, LANES), 0)
    column = lax.broadcasted_iota(jnp.int32, (16 * pieces, LANES), 1)
    piece, row = place >> 4, place & 15
    return (((row >> 1) * 16 + (row & 1) * pieces + piece) == column).astype(jnp.bfloat16)


def spare_rows(cut, pieces):
    ordered = dot(piece_order(pieces), cut, ((1,), (0,))).astype(jnp.bfloat16)
    return jnp.concatenate([ordered[16 * p : 16 * (p + 1)] for p in range(pieces)], axis=1)


def spare_cut(rows):
    pieces = rows.shape[1] // LANES
    ordered = [rows[:, LANES * p : LANES * (p + 1)] for p in range(pieces)]
    ordered = jnp.concatenate(ordered, axis=0)
    return dot(piece_order(pieces), ordered, ((0,), (0,))).astype(jnp.bfloat16)


def slot_picks(lang, slot):
    row = lax.broadcasted_iota(jnp.int32, (PART, lang.shape[1]), 0)
    is_main = row < ROWS
    block = jnp.where(is_main, row >> 4, (row - ROWS) >> 1)
    place = jnp.where(is_main, row & 15, MAIN + (row & 1))
    return ((block == lang) & (place == slot)).astype(jnp.bfloat16)


def pack_kernel(me_ref, *refs):
    sources, outs, staged, arrived = refs[:3], refs[3:7], refs[7:10], refs[10]
    copies = [
        pltpu.make_async_copy(source, stage, arrived.at[i])
        for i, (source, stage) in enumerate(zip(sources, staged))
    ]
    for copy in copies:
        copy.start()
    for copy in copies:
        copy.wait()
    width = staged[2].shape[1]
    picks = slot_picks(staged[0][...] ^ me_ref[0], staged[1][...])
    rows, cut = packed_rows(picks, staged[2][...])
    for z, out_ref in enumerate(outs):
        out_ref[:, :width] = rows[32 * z : 32 * (z + 1)]
        out_ref[:, width:] = cut[32 * z : 32 * (z + 1)]


def packed_rows(picks, values):
    rows = dot(picks, values, ((1,), (0,))).astype(jnp.bfloat16)
    return rows[:ROWS], spare_cut(rows[ROWS:])


ARRIVAL = (0, 2, 3, 1)


def split_kernel(*refs):
    messages, outs = refs[:4], refs[4:]
    for z, message_ref in zip(ARRIVAL, messages):
        for place, out_ref in enumerate(outs):
            out_ref[16 * z : 16 * (z + 1)] = message_ref[16 * place : 16 * (place + 1)]


def by_tiles(count):
    tile = min(512, count)
    return [slice(first, first + tile) for first in range(0, count, tile)]


def forward_kernel(groups, member_ref, rows_ref, up_hbm, down_hbm, *refs):
    hidden_ref, slope_ref, up_ref, down_ref = refs[:4]
    outs, arrived = refs[4:-1], refs[-1]
    tiles, width = by_tiles(up_ref.shape[1]), outs[0].shape[1]
    bands = [slice(first, first + width) for first in range(0, down_ref.shape[0], width)]
    pairs = [(up_hbm.at[:, units], up_ref.at[:, units]) for units in tiles]
    pairs += [(down_hbm.at[band], down_ref.at[band]) for band in bands]
    copies = [pltpu.make_async_copy(*pair, arrived.at[i]) for i, pair in enumerate(pairs)]
    for copy in copies:
        copy.start()
    for units, copy in zip(tiles, copies):
        copy.wait()
        pre = dot(rows_ref[...], up_ref[:, units], ((1,), (0,)))
        share = 0.5 * (1.0 + lax.erf(pre * INV_ROOT_TWO))
        hidden_ref[:, units] = (pre * share).astype(jnp.bfloat16)
        slope_ref[:, units] = share + pre * jnp.exp(-0.5 * pre * pre) * INV_ROOT_TAU
    for copy in copies[len(tiles) :]:
        copy.wait()
    for s, out_ref in enumerate(outs):
        first = pl.multiple_of(lax.rem(member_ref[0] + s, groups) * width, LANES)
        weights = down_ref[pl.ds(first, width)]
        out_ref[...] = dot(hidden_ref[...], weights, ((1,), (1,))).astype(jnp.bfloat16)


def forward(groups, member, x_rows, w_up, w_down_t):
    depth, (width, units) = x_rows.shape[0], w_up.shape
    return pl.pallas_call(
        functools.partial(forward_kernel, groups),
        out_shape=[
            pltpu.VMEM((depth, units), jnp.bfloat16),
            pltpu.VMEM((depth, units), jnp.float32),
            pltpu.VMEM(w_up.shape, w_up.dtype),
            pltpu.VMEM(w_down_t.shape, w_down_t.dtype),
        ]
        + shapes_of([(depth, width // groups)] * groups),
        in_specs=[SMEM_SPEC, VMEM_SPEC] + [pl.BlockSpec(memory_space=pltpu.HBM)] * 2,
        out_specs=[VMEM_SPEC] * (4 + groups),
        scratch_shapes=[pltpu.SemaphoreType.DMA((len(by_tiles(units)) + groups,))],
        cost_estimate=cost(FORWARD_COST),
        compiler_params=pltpu.CompilerParams(vmem_limit_bytes=10 << 20),
    )(member, x_rows, in_hbm(w_up), in_hbm(w_down_t))


def backward_kernel(rows_ref, slope_ref, up_ref, down_ref, d_pre_ref, *outs):
    for units in by_tiles(up_ref.shape[1]):
        d_hidden = dot(rows_ref[...], down_ref[:, units], ((1,), (0,)))
        d_pre_ref[:, units] = (d_hidden * slope_ref[:, units]).astype(jnp.bfloat16)
    for part in by_tiles(up_ref.shape[0]):
        share = dot(d_pre_ref[...], up_ref[part], ((1,), (1,))).astype(jnp.bfloat16)
        for g, out_ref in enumerate(outs):
            out_ref[:, part] = share[PART * g : PART * (g + 1)]


NEAR = (0, 2, 4, 6, 1, 3, 5, 7)


def put_rows(packed, rows_ref, first):
    width = rows_ref.shape[1]
    rows_ref[first : first + ROWS] = packed[:, :width]
    rows_ref[first + ROWS : first + PART] = spare_rows(packed[:, width:], width // LANES)


def unpack_near_kernel(groups, *refs):
    for g in range(groups):
        packed = jnp.concatenate([refs[g][...], refs[groups + g][...]], axis=0)
        put_rows(packed, refs[-1], PART * g)


def send_kernel(groups, me_ref, member_ref, *refs):
    sums, dx_refs, packed_ref = refs[:groups], refs[groups:-1], refs[-1]
    for s in range(groups):
        member = lax.rem(member_ref[0] + groups - s, groups)
        total = 0.0
        for t in range(groups):
            part = PART * ((s - t) % groups)
            total = total + sums[t][part : part + PART].astype(jnp.float32)
        first = 0
        for rows in (dx_refs[s][...], total.astype(jnp.bfloat16)):
            width = rows.shape[1]
            cut = spare_cut(rows[ROWS:])
            for j, near in enumerate(NEAR):
                device = (me_ref[0] ^ near) * groups + member
                at = pl.ds(pl.multiple_of(device * MAIN, MAIN), MAIN)
                main = slice(MAIN * j, MAIN * (j + 1))
                packed_ref[at, first : first + width] = rows[main]
                packed_ref[at, first + width : first + width + LANES] = cut[main]
            first += width + LANES


def collect_kernel(groups, lang_ref, slot_ref, packed_ref, out_ref, dx_ref):
    picks = slot_picks(lang_ref[...], slot_ref[...]).T
    width = dx_ref.shape[1]
    share = width // groups
    middle = width + LANES

    def blocks(g, columns):
        firsts = [MAIN * (m * groups + g) for m in range(MODULES)]
        return jnp.concatenate([packed_ref[f : f + MAIN, columns] for f in firsts], axis=0)

    def pick(main, cut):
        rows = jnp.concatenate([main, spare_rows(cut, main.shape[1] // LANES)], axis=0)
        return dot(picks, rows, ((1,), (0,))).astype(jnp.bfloat16)

    total = 0.0
    for g in range(groups):
        total = total + blocks(g, slice(0, middle)).astype(jnp.float32)
        main = blocks(g, slice(middle, middle + share))
        cut = blocks(g, slice(middle + share, middle + share + LANES))
        out_ref[:, share * g : share * (g + 1)] = pick(main, cut)
    total = total.astype(jnp.bfloat16)
    dx_ref[...] = pick(total[:, :width], total[:, width:])


def weight_grads_kernel(n_parts, start_ref, *refs):
    operands, outs, turned = refs[: 4 * n_parts], refs[4 * n_parts : -1], refs[-1]
    own, tile = outs[0].shape
    tiles = pl.num_programs(0) // 2

    for i, out_ref in enumerate(outs):
        lefts = operands[2 * n_parts * i : 2 * n_parts * i + n_parts]
        rights = operands[2 * n_parts * i + n_parts : 2 * n_parts * (i + 1)]

        @pl.when(pl.program_id(0) == i * tiles)
        def _(lefts=lefts):
            columns = pl.ds(pl.multiple_of(start_ref[0], LANES), own)
            turned[...] = jnp.concatenate([ref[:, columns] for ref in lefts], axis=0).T

        @pl.when(pl.program_id(0) // tiles == i)
        def _(i=i, rights=rights, out_ref=out_ref):
            first = (pl.program_id(0) - i * tiles) * tile
            units = pl.ds(pl.multiple_of(first, LANES), tile)
            right = jnp.concatenate([ref[:, units] for ref in rights], axis=0)
            out_ref[...] = dot(turned[...], right, ((1,), (0,))) * (1.0 / TOK_DEV)


VMEM_SPEC = pl.BlockSpec(memory_space=pltpu.VMEM)
SMEM_SPEC = pl.BlockSpec(memory_space=pltpu.SMEM)


def cost(micros):
    return pl.CostEstimate(flops=int(micros * 1e9), bytes_accessed=0, transcendentals=0)


def shapes_of(shapes):
    return [jax.ShapeDtypeStruct(shape, jnp.bfloat16) for shape in shapes]


def in_hbm(value):
    return pltpu.with_memory_space_constraint(value, pltpu.HBM)


def local(kernel, shapes, *operands, scalars=0, micros=0, grant=4, kept=()):
    outs = [s if isinstance(s, jax.ShapeDtypeStruct) else shapes_of([s])[0] for s in shapes]
    return pl.pallas_call(
        kernel,
        out_shape=[pltpu.VMEM(s.shape, s.dtype) if i in kept else s for i, s in enumerate(outs)],
        in_specs=[SMEM_SPEC] * scalars + [VMEM_SPEC] * (len(operands) - scalars),
        out_specs=[VMEM_SPEC] * len(shapes),
        cost_estimate=cost(micros),
        compiler_params=pltpu.CompilerParams(vmem_limit_bytes=grant << 20),
    )(*operands)


def pack(me, *sources):
    packed_width = sources[2].shape[1] + LANES
    return pl.pallas_call(
        pack_kernel,
        out_shape=shapes_of([(32, packed_width)] * 4),
        in_specs=[SMEM_SPEC] + [pl.BlockSpec(memory_space=pltpu.HBM)] * 3,
        out_specs=[VMEM_SPEC] * 4,
        scratch_shapes=[pltpu.VMEM(v.shape, v.dtype) for v in sources]
        + [pltpu.SemaphoreType.DMA((3,))],
        cost_estimate=cost(2),
        compiler_params=pltpu.CompilerParams(vmem_limit_bytes=4 << 20),
    )(me, *[in_hbm(v) for v in sources])


def after(values, *earlier):
    return lax.optimization_barrier((*values, *earlier))[: len(values)]


def weight_grads(start, pairs, own):
    n_parts, units = len(pairs[0][0]), pairs[0][1][0].shape[1]
    depth = sum(left.shape[0] for left in pairs[0][0])
    tile = min(512, units)
    tiles = units // tile
    if n_parts > 4:
        grads = []
        for lefts, rights in pairs:
            left = lax.dynamic_slice_in_dim(jnp.concatenate(lefts, axis=0), start, own, axis=1)
            right = jnp.concatenate(rights, axis=0)
            grads.append(dot(left, right, ((0,), (0,))) * (1.0 / TOK_DEV))
        return grads
    operands = [v for lefts, rights in pairs for v in (*lefts, *rights)]
    return pl.pallas_call(
        functools.partial(weight_grads_kernel, n_parts),
        out_shape=[jax.ShapeDtypeStruct((own, units), jnp.float32)] * 2,
        grid=(2 * tiles,),
        in_specs=[SMEM_SPEC] + [VMEM_SPEC] * len(operands),
        out_specs=[
            pl.BlockSpec((own, tile), lambda i: (0, jnp.minimum(i, tiles - 1))),
            pl.BlockSpec((own, tile), lambda i: (0, jnp.maximum(i - tiles, 0))),
        ],
        scratch_shapes=[pltpu.VMEM((own, depth), jnp.bfloat16)],
        cost_estimate=cost(4),
        compiler_params=pltpu.CompilerParams(vmem_limit_bytes=24 << 20),
    )(start.reshape(1), *operands[: 3 * n_parts], *[in_hbm(v) for v in operands[3 * n_parts :]])


def per_device(tokens, grad_out, lang_ids, slot_ids, w_up, w_down_t):
    n_lang = lax.axis_size("lang")
    n_rep = lax.axis_size("rep")
    groups = n_lang // MODULES
    count, width = tokens.shape
    lang_index = lax.axis_index("lang")
    me = (lang_index // groups).astype(jnp.int32).reshape(1)
    member = lax.rem(lang_index, groups).astype(jnp.int32).reshape(1)
    lang_row, slot_row = lang_ids.reshape(1, count), slot_ids.reshape(1, count)
    packed_width = width + LANES

    def shift_near(value, bits):
        pairs = [
            (m * groups + g, (m ^ bits) * groups + g) for m in range(MODULES) for g in range(groups)
        ]
        return lax.ppermute(value, "lang", pairs)

    def shift_group(value, step):
        pairs = [
            (m * groups + g, m * groups + (g + step) % groups)
            for m in range(MODULES)
            for g in range(groups)
        ]
        return lax.ppermute(value, "lang", pairs)

    def shift_rep(value, step):
        return lax.ppermute(value, "rep", [(r, (r + step) % n_rep) for r in range(n_rep)])

    def over_groups(value):
        return [value] + [shift_group(value, s) for s in range(1, groups)]

    def over_near(blocks, micros):
        got = [blocks[0]] + [shift_near(blocks[z], 2 * z) for z in ARRIVAL[1:]]
        return local(split_kernel, [(64, packed_width)] * 2, *got, micros=micros)

    def unpack(low, high, micros):
        return unpack_parts(over_groups(low), over_groups(high), micros)

    def unpack_parts(lows, highs, micros):
        return local(
            functools.partial(unpack_near_kernel, groups),
            [(groups * PART, width)],
            *lows,
            *highs,
            micros=micros,
            kept=(0,),
        )[0]

    messages = pack(me, lang_row, slot_row, tokens) + pack(me, lang_row, slot_row, grad_out)
    x_low, x_send = over_near(messages[:4], 0)
    y_low, y_send = over_near(messages[4:], SPLIT_COST)
    x_high, y_high = shift_near(x_send, 1), shift_near(y_send, 1)
    x_lows = over_groups(x_low)
    (x_high,) = after((x_high,), y_send, x_lows[-1])
    x_rows = unpack_parts(x_lows, over_groups(x_high), UNPACK_COST)
    y_lows, y_highs = over_groups(y_low), over_groups(y_high)
    (x_rows,) = after((x_rows,), y_high)
    y_rows = unpack_parts(y_lows, y_highs, 0)

    depth, units = groups * PART, w_up.shape[1]
    hidden, slope, w_up, w_down_t, *out_parts = forward(groups, member, x_rows, w_up, w_down_t)
    (y_rows,) = after((y_rows,), *out_parts)
    d_pre, *dx_parts = local(
        backward_kernel,
        [(depth, units)] + [(PART, width)] * groups,
        y_rows,
        slope,
        w_up,
        w_down_t,
        micros=3,
        grant=10,
        kept=(0,),
    )
    own = width // n_rep
    start = (lax.axis_index("rep") * own).astype(jnp.int32)

    def over_reps(value):
        return [value] + [shift_rep(value, s) for s in range(1, n_rep)]

    sums = [out_parts[0]] + [shift_group(out_parts[s], s) for s in range(1, groups)]
    kernel = functools.partial(send_kernel, groups)
    shape = (n_lang * MAIN, packed_width + width // groups + LANES)
    packed = local(kernel, [shape], me, member, *sums, *dx_parts, scalars=2, micros=1)[0]
    y_rows, hidden, x_rows, d_pre = after((y_rows, hidden, x_rows, d_pre), packed)
    pairs = [
        (over_reps(y_rows), over_reps(hidden)),
        (over_reps(x_rows), over_reps(d_pre)),
    ]
    grad_down, grad_up = weight_grads(start, pairs, own)
    blocks = packed.reshape(n_lang, MAIN, shape[1])
    back = lax.all_to_all(blocks, "lang", split_axis=0, concat_axis=0, tiled=True).reshape(shape)
    (back,) = after((back,), grad_down, grad_up)
    kernel = functools.partial(collect_kernel, groups)
    ffn_out, grad_tokens = local(
        kernel, [(count, width)] * 2, lang_row, slot_row, back, micros=1, grant=8
    )
    return ffn_out, grad_tokens, grad_up, grad_down


def solution(mesh):
    placed = (
        P(("lang", "rep"), None),
        P(("lang", "rep"), None),
        P(("lang", "rep")),
        P(("lang", "rep")),
        P(None, "lang"),
        P(None, "lang"),
    )
    return jax.shard_map(
        per_device,
        mesh=mesh,
        in_specs=placed,
        out_specs=(
            P(("lang", "rep"), None),
            P(("lang", "rep"), None),
            P("rep", "lang"),
            P("rep", "lang"),
        ),
        check_vma=False,
    )
```
